256 devices in a mesh: seq: 32 (over x_hi, z, core), head: 8 (over y, x_lo).
Axes of the slice: x: 4 (x_hi: 2, x_lo: 2; x = x_hi * 2 + x_lo), y: 4, z: 8, core: 2. Of those that a mesh axis runs over, the one named last changes fastest.
Arguments:
- query_rows: bfloat16 [16384, 8192], P('seq', 'head'), may hold values from -16 to 16
- key_rows: bfloat16 [16384, 1024], P('seq', 'head'), may hold values from -6 to 6
- value_rows: bfloat16 [16384, 1024], P('seq', 'head'), may hold values from -6 to 6
- out_grad: bfloat16 [16384, 8192], P('seq', 'head'), may hold values from -6 to 6
- random_blocks: int32 [128, 3], P('seq'), may hold values from 4 to 123, as said below
Outputs:
- attended: bfloat16 [16384, 8192], P('seq', 'head')
- query_grad: bfloat16 [16384, 8192], P('seq', 'head')
- key_grad: bfloat16 [16384, 1024], P('seq', 'head')
- value_grad: bfloat16 [16384, 1024], P('seq', 'head')
The draws below stay inside these ranges and needn't reach their ends.
Inputs may be any that keep to these rules, and one draw needn't show every extreme that they name: `random_blocks`: every block named for a query block lies on another index of seq than the query block, than the two indices beside it, and than the first and the last index; the 3 blocks of one query block lie on 3 different indices. Over the rows of one index of seq, at most 1 named blocks lie on any one other index, and every index names exactly 1 block of some index. The rows of the blocks 0 and 127 are not read.
All inputs are finite; a program needn't handle non-finite values.
Results may differ from the reference program's by a relative error of at most 0.019.
Values may be sent and summed in bfloat16 or wider, within the bound.
No kernel may reach another device: no remote copies, remote signals or barrier semaphores. Data moves between devices by JAX's collectives and lax.ppermute only.
A program may use at most 192 MiB of HBM per device.

```python
import math
import jax
import jax.numpy as jnp
from jax import lax

HEADS = 64
KV_HEADS = 8
D_HEAD = 128
BLOCK = 128
RANDOM = 3
QB_DEV = 4
NB = 128
TOKENS = 16384


def shared_keys(key):
    base_key = jax.random.fold_in(key, 101)
    result = jax.random.truncated_normal(base_key, -6.0, 6.0, (TOKENS, KV_HEADS * D_HEAD), jnp.float32)
    return result


def draw_key_rows(key, part):
    return shared_keys(key).astype(jnp.bfloat16)


def draw_query_rows(key, part):
    base_key = jax.random.fold_in(key, 201)
    result = jax.random.truncated_normal(base_key, -6.0, 6.0, (TOKENS, HEADS * D_HEAD), jnp.float32)
    return result.astype(jnp.bfloat16)


def draw_random_blocks(key, part):
    device_count = NB // QB_DEV
    eligible_count = device_count - 5
    slot_total = QB_DEV * RANDOM

    def per_device(device):
        order_key = jax.random.fold_in(jax.random.fold_in(key, 301), device)
        shuffled = jax.random.permutation(order_key, device_count).astype(jnp.int32)
        barred = (shuffled == device) | (shuffled == device - 1) | (shuffled == device + 1) | (shuffled == 0) | (shuffled == device_count - 1)
        ranked = jnp.argsort(barred.astype(jnp.int32), stable=True)
        eligible = shuffled[ranked][:eligible_count]
        slot_numbers = jnp.arange(slot_total, dtype=jnp.int32)
        source = eligible[slot_numbers % eligible_count]
        offset = jax.random.randint(jax.random.fold_in(order_key, 7), (slot_total,), 0, QB_DEV, dtype=jnp.int32)
        return (source * QB_DEV + offset).reshape(QB_DEV, RANDOM)
    return jax.vmap(per_device)(jnp.arange(device_count, dtype=jnp.int32)).reshape(NB, RANDOM)


def levels(rng, dims, split, smallest, high):
    def one(position, blocks):
        steps = jax.random.uniform(jax.random.fold_in(jax.random.fold_in(rng, 6), position), (blocks,), jnp.float32, smallest / len(split), high / len(split))
        return jnp.repeat(jnp.exp(steps), dims[position] // blocks).reshape((-1,) + (1,) * (len(dims) - position - 1))

    factor_of = one(*split[0])
    for cut in split[1:]:
        factor_of = factor_of * one(*cut)
    return factor_of


def normal_values(own_key, shape, scale, reach, pieces=(), held_as=jnp.bfloat16):
    values = scale * jax.random.normal(own_key, shape, jnp.float32)
    if pieces:
        values = values * levels(own_key, shape, pieces, -0.22, 0.18)
    return jnp.clip(values, -reach, reach).astype(held_as)


def setup_inputs(seed: int = 0) -> dict:
    splits = jax.random.split(jax.random.key(seed), 6)
    query_rows = draw_query_rows(jax.random.fold_in(splits[5], 71), 0)
    key_rows = draw_key_rows(jax.random.fold_in(splits[5], 71), 0)
    value_rows = normal_values(splits[2], (TOKENS, KV_HEADS * D_HEAD), 1.0, 6.0, ((0, 32), (1, 8)))
    out_grad = normal_values(splits[3], (TOKENS, HEADS * D_HEAD), 1.0, 6.0, ((0, 32), (1, 8)))
    random_blocks = draw_random_blocks(jax.random.fold_in(splits[5], 71), 0)
    return {"query_rows": query_rows, "key_rows": key_rows, "value_rows": value_rows, "out_grad": out_grad, "random_blocks": random_blocks}


def block_rows(query_block, grad_block, kv_chosen, usable):
    row_count = query_block.shape[0]
    key_width = kv_chosen.shape[-1] // 2
    key_heads = key_width // D_HEAD
    group_size = query_block.shape[1] // key_width
    slot_count = kv_chosen.shape[0]
    scaling = 1.0 / math.sqrt(D_HEAD)
    queries = query_block.astype(jnp.float32).reshape(row_count, key_heads, group_size, D_HEAD)
    upstream = grad_block.astype(jnp.float32).reshape(row_count, key_heads, group_size, D_HEAD)
    key_part = kv_chosen[..., :key_width].astype(jnp.float32).reshape(slot_count, row_count, key_heads, D_HEAD)
    value_part = kv_chosen[..., key_width:].astype(jnp.float32).reshape(slot_count, row_count, key_heads, D_HEAD)
    scores = jnp.einsum('qkgd,spkd->kgqsp', queries, key_part) * scaling
    scores = jnp.where(usable[None, None, None, :, None], scores, -jnp.inf)
    row_max = lax.optimization_barrier(jnp.max(scores, axis=(3, 4), keepdims=True))
    exponent = jnp.exp(scores - row_max)
    weights = exponent / lax.optimization_barrier(jnp.sum(exponent, axis=(3, 4), keepdims=True))
    weight_low = lax.optimization_barrier(weights.astype(jnp.bfloat16)).astype(jnp.float32)
    out_full = jnp.einsum('kgqsp,spkd->qkgd', weight_low, value_part)
    row_delta = lax.optimization_barrier(jnp.sum(upstream * out_full, axis=-1))
    weight_grad = jnp.einsum('qkgd,spkd->kgqsp', upstream, value_part)
    score_grad = weights * (weight_grad - jnp.transpose(row_delta, (1, 2, 0))[..., None, None])
    score_low = lax.optimization_barrier(score_grad.astype(jnp.bfloat16)).astype(jnp.float32)
    query_part = jnp.einsum('kgqsp,spkd->qkgd', score_low, key_part) * scaling
    key_grad = jnp.einsum('kgqsp,qkgd->spkd', score_low, queries) * scaling
    value_grad = jnp.einsum('kgqsp,qkgd->spkd', weight_low, upstream)
    contribution = jnp.concatenate([key_grad.reshape(slot_count, row_count, key_width), value_grad.reshape(slot_count, row_count, key_width)], axis=-1)
    return (out_full.reshape(row_count, -1).astype(jnp.bfloat16), query_part.reshape(row_count, -1).astype(jnp.bfloat16), contribution)

def edge_rows(edge_query, edge_upstream, key_head, value_head):
    scaling = 1.0 / math.sqrt(D_HEAD)
    highest = lax.Precision.HIGHEST
    scores = jnp.einsum('aqgd,td->agqt', edge_query, key_head, precision=highest) * scaling
    row_max = lax.optimization_barrier(jnp.max(scores, axis=-1, keepdims=True))
    exponent = jnp.exp(scores - row_max)
    weights = exponent / lax.optimization_barrier(jnp.sum(exponent, axis=-1, keepdims=True))
    out_full = jnp.einsum('agqt,td->aqgd', weights, value_head, precision=highest)
    row_delta = lax.optimization_barrier(jnp.sum(edge_upstream * out_full, axis=-1))
    weight_grad = jnp.einsum('aqgd,td->agqt', edge_upstream, value_head, precision=highest)
    score_grad = weights * (weight_grad - jnp.transpose(row_delta, (0, 2, 1))[..., None])
    query_part = jnp.einsum('agqt,td->aqgd', score_grad, key_head, precision=highest) * scaling
    key_part = jnp.einsum('agqt,aqgd->td', score_grad, edge_query, precision=highest) * scaling
    value_part = jnp.einsum('agqt,aqgd->td', weights, edge_upstream, precision=highest)
    return (out_full, query_part, key_part, value_part)

def reference(query_rows, key_rows, value_rows, out_grad, random_blocks):
    group_size = HEADS // KV_HEADS
    key_width = KV_HEADS * D_HEAD
    kv_all = jnp.concatenate([key_rows, value_rows], axis=1).reshape(NB, BLOCK, 2 * key_width)
    query_blocks = query_rows.reshape(NB, BLOCK, HEADS * D_HEAD)
    grad_blocks = out_grad.reshape(NB, BLOCK, HEADS * D_HEAD)

    def row_step(kv_grad, block_index):
        fixed = jnp.stack([block_index - 1, block_index, block_index + 1, block_index * 0, block_index * 0 + NB - 1])
        chosen = jnp.concatenate([fixed.astype(jnp.int32), random_blocks[block_index].astype(jnp.int32)])
        window_ok = jnp.stack([block_index != 1, block_index >= 0, block_index != NB - 2])
        usable = jnp.concatenate([window_ok, jnp.ones((2 + RANDOM,), jnp.bool_)])
        out_block, query_block_grad, contribution = block_rows(query_blocks[block_index], grad_blocks[block_index], kv_all[chosen], usable)
        return (kv_grad.at[chosen].add(contribution), (out_block, query_block_grad))
    kv_grad, (middle_out, middle_query) = lax.scan(row_step, jnp.zeros(kv_all.shape, jnp.float32), jnp.arange(1, NB - 1, dtype=jnp.int32))
    edge_pick = jnp.stack([jnp.zeros((), jnp.int32), jnp.full((), NB - 1, jnp.int32)])
    edge_query = query_blocks[edge_pick].astype(jnp.float32).reshape(2, BLOCK, KV_HEADS, group_size, D_HEAD).transpose(2, 0, 1, 3, 4)
    edge_upstream = grad_blocks[edge_pick].astype(jnp.float32).reshape(2, BLOCK, KV_HEADS, group_size, D_HEAD).transpose(2, 0, 1, 3, 4)
    key_heads_all = key_rows.astype(jnp.float32).reshape(NB * BLOCK, KV_HEADS, D_HEAD).transpose(1, 0, 2)
    value_heads_all = value_rows.astype(jnp.float32).reshape(NB * BLOCK, KV_HEADS, D_HEAD).transpose(1, 0, 2)

    def per_head(operands):
        return edge_rows(operands[0], operands[1], operands[2], operands[3])
    edge_out, edge_query_grad, edge_key_grad, edge_value_grad = lax.map(per_head, (edge_query, edge_upstream, key_heads_all, value_heads_all))
    edge_attended = edge_out.transpose(1, 2, 0, 3, 4).reshape(2, BLOCK, HEADS * D_HEAD).astype(jnp.bfloat16)
    edge_qflat = edge_query_grad.transpose(1, 2, 0, 3, 4).reshape(2, BLOCK, HEADS * D_HEAD).astype(jnp.bfloat16)
    attended = jnp.concatenate([edge_attended[0:1], middle_out, edge_attended[1:2]], axis=0).reshape(NB * BLOCK, HEADS * D_HEAD)
    query_grad = jnp.concatenate([edge_qflat[0:1], middle_query, edge_qflat[1:2]], axis=0).reshape(NB * BLOCK, HEADS * D_HEAD)
    flat_grad = kv_grad.reshape(NB * BLOCK, 2 * key_width)
    key_grad = flat_grad[:, :key_width] + edge_key_grad.transpose(1, 0, 2).reshape(NB * BLOCK, key_width)
    value_grad = flat_grad[:, key_width:] + edge_value_grad.transpose(1, 0, 2).reshape(NB * BLOCK, key_width)
    return (attended, query_grad, key_grad.astype(jnp.bfloat16), value_grad.astype(jnp.bfloat16))
```

```python
import math

import jax
import jax.numpy as jnp
from jax import lax
from jax.experimental import pallas as pl
from jax.experimental.pallas import tpu as pltpu
from jax.sharding import PartitionSpec as P

D = 128
B = 128
SEQ = 32
ZN = 8
QB = 4
NB = SEQ * QB
HEADS = 8
ROWS = QB * B
PIECE = ROWS + 16
SLOTS = 8
KEYS = SLOTS * B
SCALE = 1.0 / math.sqrt(D)
LOG2E = math.log2(math.e)
FAR = -1e30
VMEM_LIMIT = 56 * 1024 * 1024
NT = (((1,), (1,)), ((), ()))
TN = (((0,), (0,)), ((), ()))


def device_of(x, z, c):
    return x * 16 + (z % ZN) * 2 + c


ALL = [(x, z, c) for x in range(2) for z in range(ZN) for c in range(2)]


def along_z(step):
    return [(device_of(x, z, c), device_of(x, z + step, c)) for x, z, c in ALL]


CORE = [(i, i ^ 1) for i in range(SEQ)]
ACROSS = [(i, i ^ 16) for i in range(SEQ)]
EDGE_Z = (0, ZN - 1)
EDGE_ACROSS = [(0, 16), (31, 15)]


def edge_tree(step):
    pairs = []
    for x in range(2):
        for c, sign in ((0, 1), (1, -1)):
            for r in range(0, ZN, 2 * step):
                ends = [EDGE_Z[c] + sign * r, EDGE_Z[c] + sign * (r + step)]
                pairs.append(tuple(device_of(x, z, c) for z in ends))
    return pairs


def swap_z(bit):
    return [(device_of(x, z, c), device_of(x, z ^ bit, c)) for x, z, c in ALL]


def reverse(pairs):
    return [(b, a) for a, b in pairs]


def permute(value, pairs):
    return lax.ppermute(value, "seq", pairs)


def dot(a, b, dims=(((1,), (0,)), ((), ()))):
    return lax.dot_general(a, b, dims, preferred_element_type=jnp.float32)


def two_heads(ref_value, first):
    return jnp.concatenate(
        [ref_value[:, first : first + D], ref_value[:, first + D : first + 2 * D]], axis=0
    )


def edge_stats_kernel(edge_ref, k0, k1, k2, k3, stats_ref):
    stats_ref[...] = jnp.zeros_like(stats_ref)
    for pair in range(2):
        q2 = two_heads(edge_ref, pair * 2 * D)
        g2 = two_heads(edge_ref, 4 * D + pair * 2 * D)
        scores = [dot(k[:ROWS, :D], q2, NT) * (SCALE * LOG2E) for k in (k0, k1, k2, k3)]
        top = scores[0].max(axis=0, keepdims=True)
        for s in scores[1:]:
            top = jnp.maximum(top, s.max(axis=0, keepdims=True))
        total = jnp.zeros_like(top)
        delta = jnp.zeros_like(top)
        for s, k in zip(scores, (k0, k1, k2, k3)):
            e = jnp.exp2(s - top)
            total = total + e.sum(axis=0, keepdims=True)
            w = dot(k[:ROWS, D:], g2, NT)
            delta = delta + (e * w).sum(axis=0, keepdims=True)
        cols = slice(pair * 2 * D, (pair + 1) * 2 * D)
        stats_ref[0:1, cols] = top
        stats_ref[1:2, cols] = total
        stats_ref[2:3, cols] = delta


def edge_grad_kernel(
    edge_ref, k0, k1, k2, k3, stats_ref, oq_ref, own_ref, core_ref, across_ref
):
    total = stats_ref[1:2]
    delta = stats_ref[2:3] / total
    shift = stats_ref[0:1] + jnp.log2(total)
    q_all = jnp.concatenate([two_heads(edge_ref, 0), two_heads(edge_ref, 2 * D)], axis=0)
    g_all = jnp.concatenate([two_heads(edge_ref, 4 * D), two_heads(edge_ref, 6 * D)], axis=0)
    out = None
    for n, k in enumerate((k0, k1, k2, k3)):
        keys = k[:ROWS, :D]
        values = k[:ROWS, D:]
        p = jnp.exp2(dot(keys, q_all, NT) * (SCALE * LOG2E) - shift)
        ds = (p * (dot(values, g_all, NT) - delta)).astype(jnp.bfloat16)
        p = p.astype(jnp.bfloat16)
        o = dot(values, p, TN)
        dq = dot(keys, ds, TN)
        out = (o, dq) if out is None else (out[0] + o, out[1] + dq)
        dk = dot(ds, q_all) * SCALE
        dv = dot(p, g_all)
        if n == 0:
            own_ref[:, :D] = dk
            own_ref[:, D:] = dv
        elif n == 1:
            across_ref[:, :D] = dk
            across_ref[:, D:] = dv
        else:
            core_ref[n - 2, :, :D] = dk.astype(jnp.bfloat16)
            core_ref[n - 2, :, D:] = dv.astype(jnp.bfloat16)
    for h in range(4):
        cols = slice(h * D, (h + 1) * D)
        oq_ref[:, cols] = out[0][:, cols].T.astype(jnp.bfloat16)
        oq_ref[:, 4 * D + h * D : 4 * D + (h + 1) * D] = (out[1][:, cols].T * SCALE).astype(
            jnp.bfloat16
        )


def middle_kernel(info, q_ref, g_ref, *refs):
    pieces = refs[:SEQ]
    out_ref, dq_ref, send_ref, extra_ref, own_ref, ids_ref = refs[SEQ + 1 : SEQ + 7]
    kv, p_all, ds_all, dk_ref, dv_ref, first_acc, last_acc = refs[SEQ + 7 :]
    for n, piece in enumerate(pieces):
        ids_ref[n] = piece[ROWS:PIECE, :]
    me = info[12]
    my_x, my_z, my_c = me >> 4, (me >> 1) & 7, me & 1

    own_ref[...] = jnp.zeros_like(own_ref)
    first_acc[...] = jnp.zeros_like(first_acc)
    last_acc[...] = jnp.zeros_like(last_acc)
    extra_ref[...] = jnp.zeros_like(extra_ref)

    def fetch(block, slot):
        src = block >> 2
        offset = pl.multiple_of((block & 3) * B, B)
        rel_z = ((src >> 1) - my_z) & 7
        low = (((src >> 4) ^ my_x) << 1) | ((src & 1) ^ my_c)
        for a in range(ZN):

            @pl.when(rel_z == a)
            def _():
                for b in range(4):

                    @pl.when(low == b)
                    def _():
                        kv[slot * B : (slot + 1) * B, :] = pieces[a * 4 + b][pl.ds(offset, B), :]

    def contribution(slot):
        rows = slice(slot * B, (slot + 1) * B)
        return jnp.concatenate([dk_ref[rows, :], dv_ref[rows, :]], axis=1)

    def one_block(j, carry):
        block = me * QB + j
        middle = jnp.logical_and(block > 0, block < NB - 1)

        @pl.when(middle)
        def _():
            fetch(block - 1, 0)
            fetch(block, 1)
            fetch(block + 1, 2)
            fetch(0, 3)
            fetch(NB - 1, 4)
            for r in range(3):
                fetch(info[j * 3 + r], 5 + r)
            rows = pl.ds(pl.multiple_of(j * B, B), B)
            low_bias = jnp.where(block == 1, FAR, 0.0).astype(jnp.float32)
            high_bias = jnp.where(block == NB - 2, FAR, 0.0).astype(jnp.float32)
            slot_of = lax.broadcasted_iota(jnp.int32, (KEYS, 1), 0) // B
            bias = jnp.where(slot_of == 0, low_bias, jnp.where(slot_of == 2, high_bias, 0.0))
            keys = kv[:, :D]
            values = kv[:, D:]
            q = q_ref[rows, :]
            g = g_ref[rows, :]
            for pair in range(HEADS // 2):
                cols = slice(pair * 2 * D, (pair + 1) * 2 * D)
                q2 = two_heads(q, pair * 2 * D)
                g2 = two_heads(g, pair * 2 * D)
                s = dot(keys, q2, NT) * (SCALE * LOG2E) + bias
                e = jnp.exp2(s - s.max(axis=0, keepdims=True))
                p = e * (1.0 / e.sum(axis=0, keepdims=True))
                p_low = p.astype(jnp.bfloat16)
                p_all[:, cols] = p_low
                out = dot(values, p_low, TN).T
                delta = (g2.astype(jnp.float32) * out).T.sum(axis=0, keepdims=True)
                ds = (p * (dot(values, g2, NT) - delta)).astype(jnp.bfloat16)
                ds_all[:, cols] = ds
                dq = dot(keys, ds, TN).T * SCALE
                for h in range(2):
                    part = slice((pair * 2 + h) * D, (pair * 2 + h + 1) * D)
                    out_ref[rows, part] = out[h * B : (h + 1) * B].astype(jnp.bfloat16)
                    dq_ref[rows, part] = dq[h * B : (h + 1) * B].astype(jnp.bfloat16)
            q_all = jnp.concatenate([q[:, h * D : (h + 1) * D] for h in range(HEADS)], axis=0)
            g_all = jnp.concatenate([g[:, h * D : (h + 1) * D] for h in range(HEADS)], axis=0)
            dk_ref[...] = dot(ds_all[...], q_all) * SCALE
            dv_ref[...] = dot(p_all[...], g_all)

            own_ref[rows, :] += contribution(1)
            first_acc[...] += contribution(3)
            last_acc[...] += contribution(4)

            @pl.when(j > 0)
            def _():
                own_ref[pl.ds(pl.multiple_of((j - 1) * B, B), B), :] += contribution(0)

            @pl.when(j < QB - 1)
            def _():
                own_ref[pl.ds(pl.multiple_of((j + 1) * B, B), B), :] += contribution(2)

            @pl.when(jnp.logical_and(j == 0, me != 1))
            def _():
                send_ref[me - 1] = contribution(0).astype(jnp.bfloat16)

            @pl.when(jnp.logical_and(j == 0, me == 1))
            def _():
                extra_ref[...] = contribution(0).astype(jnp.bfloat16)

            @pl.when(jnp.logical_and(j == QB - 1, me != SEQ - 2))
            def _():
                send_ref[me + 1] = contribution(2).astype(jnp.bfloat16)

            @pl.when(jnp.logical_and(j == QB - 1, me == SEQ - 2))
            def _():
                extra_ref[...] = contribution(2).astype(jnp.bfloat16)

            for r in range(3):
                send_ref[info[j * 3 + r] >> 2] = contribution(5 + r).astype(jnp.bfloat16)

        return carry

    lax.fori_loop(0, QB, one_block, 0)

    @pl.when(me == 0)
    def _():
        own_ref[:B, :] += first_acc[...]

    @pl.when(me != 0)
    def _():
        send_ref[0] = first_acc[...].astype(jnp.bfloat16)

    @pl.when(me == SEQ - 1)
    def _():
        own_ref[ROWS - B :, :] += last_acc[...]

    @pl.when(me != SEQ - 1)
    def _():
        send_ref[SEQ - 1] = last_acc[...].astype(jnp.bfloat16)


def sum_kernel(
    target, recv_ref, extra_ref, own_ref, edge_ref, edge_core_ref, edge_across_ref, dk_ref, dv_ref, acc
):
    acc[...] = (
        own_ref[...]
        + edge_ref[...]
        + edge_core_ref[0].astype(jnp.float32)
        + edge_across_ref[...].astype(jnp.float32)
    )

    def add(s, carry):
        t = target[s]

        @pl.when(t >= 0)
        def _():
            rows = pl.ds(pl.multiple_of(t * B, B), B)
            acc[rows, :] += recv_ref[s].astype(jnp.float32)

        return carry

    lax.fori_loop(0, SEQ, add, 0)
    t = target[SEQ]

    @pl.when(t >= 0)
    def _():
        rows = pl.ds(pl.multiple_of(t * B, B), B)
        acc[rows, :] += extra_ref[...].astype(jnp.float32)

    dk_ref[...] = acc[:, :D].astype(jnp.bfloat16)
    dv_ref[...] = acc[:, D:].astype(jnp.bfloat16)


def call(kernel, outs, args, scalars=0, later=0, scratch=(), flops=0, bytes_accessed=0, exps=0):
    vmem = pl.BlockSpec(memory_space=pltpu.VMEM)
    smem = pl.BlockSpec(memory_space=pltpu.SMEM)
    return pl.pallas_call(
        kernel,
        out_shape=[jax.ShapeDtypeStruct(shape, dtype) for shape, dtype in outs],
        in_specs=[smem] * scalars
        + [vmem] * (len(args) - scalars - later)
        + [pl.BlockSpec(memory_space=pl.ANY)] * later,
        out_specs=[vmem] * len(outs),
        scratch_shapes=list(scratch),
        compiler_params=pltpu.CompilerParams(vmem_limit_bytes=VMEM_LIMIT),
        cost_estimate=pl.CostEstimate(
            flops=flops, bytes_accessed=bytes_accessed, transcendentals=exps
        ),
    )(*args)


def gather_pieces(mine):
    half = PIECE // 2
    columns = []
    for start in (mine, permute(mine, ACROSS)):
        by_z = [start] + [None] * (ZN - 1)
        up = down = start
        for step in range(1, ZN // 2):
            up = permute(up, along_z(1))
            down = permute(down, along_z(-1))
            by_z[ZN - step] = up
            by_z[step] = down
        up = permute(up[:half], along_z(1))
        down = permute(down[half:], along_z(-1))
        by_z[ZN // 2] = jnp.concatenate([up, down], axis=0)
        columns.append(by_z)
    pieces = []
    for z in range(ZN):
        for x in range(2):
            pieces += [columns[x][z], permute(columns[x][z], CORE)]
    return pieces


def local(query_rows, key_rows, value_rows, out_grad, random_blocks):
    bf16, f32 = jnp.bfloat16, jnp.float32
    me = lax.axis_index("seq").astype(jnp.int32)
    my_x, my_z, my_c = me >> 4, (me >> 1) & 7, me & 1
    ids = random_blocks.reshape(QB * 3).astype(jnp.int32)

    at_edge = my_z == jnp.where(my_c == 0, EDGE_Z[0], EDGE_Z[1])
    is_root = jnp.logical_or(me == 0, me == SEQ - 1)
    edge_start = my_c * (ROWS - B)

    def edge_half(x):
        return jnp.concatenate(
            [
                lax.dynamic_slice(rows, (edge_start, x * (4 * D)), (B, 4 * D))
                for rows in (query_rows, out_grad)
            ],
            axis=1,
        )

    arrived = permute(edge_half(1 - my_x), EDGE_ACROSS)
    edge_here = jnp.where(is_root, edge_half(my_x), arrived)
    edge_here = jnp.where(at_edge, edge_here, jnp.zeros_like(edge_here))
    edge = edge_here
    for step in (4, 2, 1):
        edge = edge + permute(edge, edge_tree(step))

    id_rows = jnp.zeros((PIECE - ROWS, 2 * D), bf16).at[0, : QB * 3].set(ids.astype(bf16))
    mine = jnp.concatenate(
        [jnp.concatenate([key_rows, value_rows], axis=1), id_rows], axis=0
    )
    pieces = gather_pieces(mine)
    near = [pieces[0], pieces[2], pieces[1], pieces[3]]

    edge_flops = 2 * 4 * ROWS * ROWS * D
    (stats,) = call(
        edge_stats_kernel,
        [((8, 4 * D), f32)],
        [edge] + near,
        flops=2 * edge_flops,
        bytes_accessed=2 << 20,
        exps=4 * ROWS * ROWS,
    )
    for bit in (1, 2, 4):
        other = permute(stats, swap_z(bit))
        top = jnp.maximum(stats[0:1], other[0:1])
        joined = stats * jnp.exp2(stats[0:1] - top) + other * jnp.exp2(other[0:1] - top)
        stats = jnp.concatenate([top, joined[1:]], axis=0)
    edge_oq, edge_own, edge_core, edge_across = call(
        edge_grad_kernel,
        [
            ((B, 8 * D), bf16),
            ((ROWS, 2 * D), f32),
            ((2, ROWS, 2 * D), bf16),
            ((ROWS, 2 * D), f32),
        ],
        [edge] + near + [stats],
        flops=6 * edge_flops,
        bytes_accessed=4 << 20,
        exps=4 * ROWS * ROWS,
    )
    edge_core = permute(edge_core, CORE)
    edge_across = permute((edge_across + edge_core[1].astype(f32)).astype(bf16), ACROSS)
    oq_sum = edge_oq.astype(f32)
    for step in (1, 2, 4):
        part = permute(oq_sum.astype(bf16), reverse(edge_tree(step)))
        oq_sum = oq_sum + part.astype(f32)
    oq_here = oq_sum.astype(bf16)
    oq_other = permute(oq_here, reverse(EDGE_ACROSS))

    info = jnp.concatenate([ids, me[None], jnp.zeros((3,), jnp.int32)])
    attended, query_grad, send, extra, own, ids_of = call(
        middle_kernel,
        [
            ((ROWS, HEADS * D), bf16),
            ((ROWS, HEADS * D), bf16),
            ((SEQ, B, 2 * D), bf16),
            ((B, 2 * D), bf16),
            ((ROWS, 2 * D), f32),
            ((SEQ, PIECE - ROWS, 2 * D), bf16),
        ],
        [info, query_rows, out_grad] + pieces + [edge_oq],
        scalars=1,
        later=1,
        scratch=[
            pltpu.VMEM((KEYS, 2 * D), bf16),
            pltpu.VMEM((KEYS, HEADS * B), bf16),
            pltpu.VMEM((KEYS, HEADS * B), bf16),
            pltpu.VMEM((KEYS, D), f32),
            pltpu.VMEM((KEYS, D), f32),
            pltpu.VMEM((B, 2 * D), f32),
            pltpu.VMEM((B, 2 * D), f32),
        ],
        flops=QB * 6 * 2 * KEYS * HEADS * B * D,
        bytes_accessed=16 << 20,
        exps=QB * KEYS * HEADS * B,
    )
    recv = lax.all_to_all(send, "seq", 0, 0)
    extra = permute(extra, [(1, 0), (SEQ - 2, SEQ - 1)])

    table = ids_of[:, 0, : QB * 3].astype(jnp.int32)
    place = jnp.arange(SEQ, dtype=jnp.int32)
    source = (
        ((((place & 3) >> 1) ^ my_x) << 4) | (((my_z + (place >> 2)) & 7) << 1) | ((place & 1) ^ my_c)
    )
    row = source[:, None] * QB + jnp.arange(QB * 3, dtype=jnp.int32)[None, :] // 3
    read = jnp.logical_and(row > 0, row < NB - 1)
    mine_named = jnp.logical_and((table >> 2) == me, read)
    named = jnp.max(jnp.where(mine_named, table & 3, -1), axis=1)
    named = jnp.where(source == me - 1, 0, jnp.where(source == me + 1, QB - 1, named))
    named = jnp.where(me == 0, 0, jnp.where(me == SEQ - 1, QB - 1, named))
    named = jnp.where(source == me, -1, named)
    by_source = jnp.max(
        jnp.where(source[None, :] == place[:, None], named[None, :], -1), axis=1
    )
    extra_at = jnp.where(me == 0, QB - 1, jnp.where(me == SEQ - 1, 0, -1))
    target = jnp.concatenate([by_source, extra_at[None]]).astype(jnp.int32)

    key_grad, value_grad = call(
        sum_kernel,
        [((ROWS, D), bf16), ((ROWS, D), bf16)],
        [target, recv, extra, own, edge_own, edge_core, edge_across],
        scalars=1,
        scratch=[pltpu.VMEM((ROWS, 2 * D), f32)],
        flops=1 << 20,
        bytes_accessed=4 << 20,
    )

    low = jnp.where(my_x == 0, oq_here, oq_other)
    high = jnp.where(my_x == 0, oq_other, oq_here)

    def put(whole, start):
        edge_rows = jnp.concatenate(
            [low[:, start : start + 4 * D], high[:, start : start + 4 * D]], axis=1
        )
        present = lax.dynamic_slice(whole, (edge_start, 0), (B, HEADS * D))
        return lax.dynamic_update_slice(
            whole, jnp.where(is_root, edge_rows, present), (edge_start, 0)
        )

    return put(attended, 0), put(query_grad, 4 * D), key_grad, value_grad


def solution(mesh):
    rows = P("seq", "head")
    return jax.shard_map(
        local,
        mesh=mesh,
        in_specs=(rows, rows, rows, rows, P("seq", None)),
        out_specs=(rows, rows, rows, rows),
        check_vma=False,
    )
```

```python
import functools
import math

import jax
import jax.numpy as jnp
from jax import lax
from jax.experimental import pallas as pl
from jax.experimental.pallas import tpu as pltpu
from jax.sharding import PartitionSpec as P

D = 128
B = 128
SEQ = 32
ZN = 8
QB = 4
NB = SEQ * QB
HEADS = 8
ROWS = QB * B
PIECE = ROWS + 16
SLOTS = 8
KEYS = SLOTS * B
SCALE = 1.0 / math.sqrt(D)
LOG2E = math.log2(math.e)
FAR = -1e30
VMEM_LIMIT = 56 * 1024 * 1024
NT = (((1,), (1,)), ((), ()))
TN = (((0,), (0,)), ((), ()))


def device_of(x, z, c):
    return x * 16 + (z % ZN) * 2 + c


ALL = [(x, z, c) for x in range(2) for z in range(ZN) for c in range(2)]


CORE = [(i, i ^ 1) for i in range(SEQ)]
ACROSS = [(i, i ^ 16) for i in range(SEQ)]
Z_GROUPS = [[device_of(x, z, c) for z in range(ZN)] for x in range(2) for c in range(2)]
ZC_GROUPS = [[device_of(x, z, c) for z in range(ZN) for c in range(2)] for x in range(2)]
EDGE_Z = (0, ZN - 1)
EDGE_ACROSS = [(0, 16), (31, 15)]


def edge_tree(step):
    pairs = []
    for x in range(2):
        for c, sign in ((0, 1), (1, -1)):
            for r in range(0, ZN, 2 * step):
                ends = [EDGE_Z[c] + sign * r, EDGE_Z[c] + sign * (r + step)]
                pairs.append(tuple(device_of(x, z, c) for z in ends))
    return pairs


def to_edge(step):
    return [
        (device_of(x, EDGE_Z[c] + step, c), device_of(x, EDGE_Z[c], c))
        for x in range(2)
        for c in range(2)
    ]


def reverse(pairs):
    return [(b, a) for a, b in pairs]


def place_of(source, my_x):
    return ((source & 15) << 1) | ((source >> 4) ^ my_x)


def permute(value, pairs):
    return lax.ppermute(value, "seq", pairs)


def dot(a, b, dims=(((1,), (0,)), ((), ()))):
    return lax.dot_general(a, b, dims, preferred_element_type=jnp.float32)


def two_heads(ref_value, first):
    return jnp.concatenate(
        [ref_value[:, first : first + D], ref_value[:, first + D : first + 2 * D]], axis=0
    )


def edge_stats_kernel(edge_ref, k0, k1, k2, k3, stats_ref):
    stats_ref[...] = jnp.zeros_like(stats_ref)
    for pair in range(2):
        q2 = two_heads(edge_ref, pair * 2 * D)
        g2 = two_heads(edge_ref, 4 * D + pair * 2 * D)
        scores = [dot(k[:ROWS, :D], q2, NT) * (SCALE * LOG2E) for k in (k0, k1, k2, k3)]
        top = scores[0].max(axis=0, keepdims=True)
        for s in scores[1:]:
            top = jnp.maximum(top, s.max(axis=0, keepdims=True))
        total = jnp.zeros_like(top)
        delta = jnp.zeros_like(top)
        for s, k in zip(scores, (k0, k1, k2, k3)):
            e = jnp.exp2(s - top)
            total = total + e.sum(axis=0, keepdims=True)
            w = dot(k[:ROWS, D:], g2, NT)
            delta = delta + (e * w).sum(axis=0, keepdims=True)
        cols = slice(pair * 2 * D, (pair + 1) * 2 * D)
        stats_ref[0:1, cols] = top
        stats_ref[1:2, cols] = total
        stats_ref[2:3, cols] = delta


def edge_grad_kernel(
    edge_ref, k0, k1, k2, k3, stats_ref, oq_ref, own_ref, core_ref, across_ref
):
    stats = [stats_ref[n] for n in range(ZN)]
    top = stats[0][0:1]
    for s in stats[1:]:
        top = jnp.maximum(top, s[0:1])
    total = jnp.zeros_like(top)
    delta = jnp.zeros_like(top)
    for s in stats:
        factor = jnp.exp2(s[0:1] - top)
        total = total + s[1:2] * factor
        delta = delta + s[2:3] * factor
    delta = delta / total
    shift = top + jnp.log2(total)
    q_all = jnp.concatenate([two_heads(edge_ref, 0), two_heads(edge_ref, 2 * D)], axis=0)
    g_all = jnp.concatenate([two_heads(edge_ref, 4 * D), two_heads(edge_ref, 6 * D)], axis=0)
    out = None
    for n, k in enumerate((k0, k1, k2, k3)):
        keys = k[:ROWS, :D]
        values = k[:ROWS, D:]
        p = jnp.exp2(dot(keys, q_all, NT) * (SCALE * LOG2E) - shift)
        ds = (p * (dot(values, g_all, NT) - delta)).astype(jnp.bfloat16)
        p = p.astype(jnp.bfloat16)
        o = dot(values, p, TN)
        dq = dot(keys, ds, TN)
        out = (o, dq) if out is None else (out[0] + o, out[1] + dq)
        dk = dot(ds, q_all) * SCALE
        dv = dot(p, g_all)
        if n == 0:
            own_ref[:, :D] = dk
            own_ref[:, D:] = dv
        elif n == 1:
            across_ref[:, :D] = dk
            across_ref[:, D:] = dv
        else:
            core_ref[n - 2, :, :D] = dk.astype(jnp.bfloat16)
            core_ref[n - 2, :, D:] = dv.astype(jnp.bfloat16)
    for h in range(4):
        cols = slice(h * D, (h + 1) * D)
        oq_ref[:, cols] = out[0][:, cols].T.astype(jnp.bfloat16)
        oq_ref[:, 4 * D + h * D : 4 * D + (h + 1) * D] = (out[1][:, cols].T * SCALE).astype(
            jnp.bfloat16
        )


def middle_kernel(info, q_ref, g_ref, all_ref, _, *refs):
    out_ref, dq_ref, send_ref, state_ref, side_ref = refs[:5]
    kv, s_ref, e_all, ds_all, slots, sems, slot_sems = refs[5:]
    me = info[12]
    j = pl.program_id(0)
    last_step = j == QB - 1

    def fetch(block, buffer, slot):
        block = jnp.clip(block, 0, NB - 1)
        place = place_of(block >> 2, me >> 4)
        row = pl.multiple_of(place * PIECE + (block & 3) * B, 16)
        return pltpu.make_async_copy(
            all_ref.at[pl.ds(row, B), :], kv.at[buffer, pl.ds(slot * B, B), :], sems.at[buffer, slot]
        )

    def slot_copy(at, which, destination):
        return pltpu.make_async_copy(
            slots.at[at, which], send_ref.at[destination], slot_sems.at[at, which]
        )

    def fetch_all(step, buffer):
        block = me * QB + step
        for slot, name in enumerate((block - 1, block, block + 1, 0, NB - 1)):
            fetch(jnp.int32(name), buffer, slot).start()
        for r in range(3):
            fetch(info[step * 3 + r], buffer, 5 + r).start()

    @pl.when(j == 0)
    def _():
        fetch_all(0, 0)
        state_ref[...] = jnp.zeros_like(state_ref)
        side_ref[...] = jnp.zeros_like(side_ref)

    buffer = j & 1

    @pl.when(jnp.logical_not(last_step))
    def _():
        fetch_all(j + 1, 1 - buffer)

    for slot in range(SLOTS):
        fetch(jnp.int32(0), buffer, slot).wait()

    block = me * QB + j
    middle = jnp.logical_and(block > 0, block < NB - 1)
    to_low = jnp.logical_and(jnp.logical_and(middle, j == 0), me != 1)
    to_high = jnp.logical_and(jnp.logical_and(middle, j == QB - 1), me != SEQ - 2)

    @pl.when(middle)
    def _():
        low_bias = jnp.where(block == 1, FAR, 0.0).astype(jnp.float32)
        high_bias = jnp.where(block == NB - 2, FAR, 0.0).astype(jnp.float32)
        values_t = kv[buffer, :, D:].T
        keys_t = kv[buffer, :, :D].T
        scaled_q, scaled_g = [], []
        pairs = range(HEADS // 2)
        heads = [[slice((2 * p + h) * D, (2 * p + h + 1) * D) for h in range(2)] for p in pairs]
        chunks = [slice(n * B, (n + 1) * B) for n in range(KEYS // B)]

        def scores(pair):
            q_t = jnp.concatenate([q_ref[:, h].T for h in heads[pair]], axis=1)
            top = None
            for n, c in enumerate(chunks):
                s = dot(kv[buffer, c, :D], q_t)
                if n == 0:
                    s = s + low_bias
                if n == 2:
                    s = s + high_bias
                s_ref[pair % 2, c, :] = s
                m = s.max(axis=0, keepdims=True)
                top = m if top is None else jnp.maximum(top, m)
            return top * (SCALE * LOG2E)

        def weights(pair, top):
            cols = slice(pair * 2 * D, (pair + 1) * 2 * D)
            total = None
            for c in chunks:
                e = jnp.exp2(s_ref[pair % 2, c, :] * (SCALE * LOG2E) - top)
                e_all[c, cols] = e.astype(jnp.bfloat16)
                t = e.sum(axis=0, keepdims=True)
                total = t if total is None else total + t
            return 1.0 / total

        def gradients(pair, part):
            cols = slice(pair * 2 * D, (pair + 1) * 2 * D)
            g_t = jnp.concatenate([g_ref[:, h].T for h in heads[pair]], axis=1)
            o = dot(values_t, e_all[:, cols]) * part
            delta = (g_t.astype(jnp.float32) * o).sum(axis=0, keepdims=True)
            for c in chunks:
                e = e_all[c, cols].astype(jnp.float32)
                ds_all[c, cols] = (e * (dot(kv[buffer, c, D:], g_t) - delta)).astype(jnp.bfloat16)
            dq = dot(keys_t, ds_all[:, cols]) * (part * SCALE)
            for n, h in enumerate(heads[pair]):
                one = slice(n * B, (n + 1) * B)
                out_ref[:, h] = o[:, one].T.astype(jnp.bfloat16)
                dq_ref[:, h] = dq[:, one].T.astype(jnp.bfloat16)
                column = part[:, one].T
                scaled_q.append((q_ref[:, h] * (column * SCALE)).astype(jnp.bfloat16))
                scaled_g.append((g_ref[:, h] * column).astype(jnp.bfloat16))

        top = scores(0)
        for pair in pairs:
            part = weights(pair, top)
            if pair + 1 < HEADS // 2:
                top = scores(pair + 1)
            gradients(pair, part)
        dk = dot(ds_all[...], jnp.concatenate(scaled_q, axis=0))
        dv = dot(e_all[...], jnp.concatenate(scaled_g, axis=0))

        def contribution(slot):
            rows = slice(slot * B, (slot + 1) * B)
            return jnp.concatenate([dk[rows], dv[rows]], axis=1)

        def low(slot):
            return contribution(slot).astype(jnp.bfloat16)

        state_ref[pl.ds(pl.multiple_of(j * B, B), B), :] += contribution(1)
        state_ref[ROWS : ROWS + B, :] += contribution(3)
        state_ref[ROWS + B :, :] += contribution(4)

        @pl.when(j > 0)
        def _():
            state_ref[pl.ds(pl.multiple_of((j - 1) * B, B), B), :] += contribution(0)

        @pl.when(j < QB - 1)
        def _():
            state_ref[pl.ds(pl.multiple_of((j + 1) * B, B), B), :] += contribution(2)

        for r in range(3):
            slots[j, r] = low(5 + r)
            slot_copy(j, r, info[j * 3 + r] >> 2).start()

        @pl.when(j == 0)
        def _():
            slots[j, 3] = low(0)

        @pl.when(j == QB - 1)
        def _():
            slots[j, 3] = low(2)

        @pl.when(to_low)
        def _():
            slot_copy(j, 3, me - 1).start()

        @pl.when(to_high)
        def _():
            slot_copy(j, 3, me + 1).start()

        @pl.when(jnp.logical_and(j == 0, me == 1))
        def _():
            side_ref[...] = low(0)

        @pl.when(jnp.logical_and(j == QB - 1, me == SEQ - 2))
        def _():
            side_ref[...] = low(2)

    @pl.when(last_step)
    def _():
        slots[QB, 0] = state_ref[ROWS : ROWS + B, :].astype(jnp.bfloat16)
        slots[QB, 1] = state_ref[ROWS + B :, :].astype(jnp.bfloat16)

        @pl.when(me == 0)
        def _():
            state_ref[:B, :] += state_ref[ROWS : ROWS + B, :]

        @pl.when(me != 0)
        def _():
            slot_copy(QB, 0, 0).start()
            slot_copy(QB, 0, 0).wait()

        @pl.when(me == SEQ - 1)
        def _():
            state_ref[ROWS - B : ROWS, :] += state_ref[ROWS + B :, :]

        @pl.when(me != SEQ - 1)
        def _():
            slot_copy(QB, 1, SEQ - 1).start()
            slot_copy(QB, 1, SEQ - 1).wait()

    @pl.when(middle)
    def _():
        for r in range(3):
            slot_copy(j, r, 0).wait()

    @pl.when(jnp.logical_or(to_low, to_high))
    def _():
        slot_copy(j, 3, 0).wait()


def middle_call(info, query_rows, out_grad, gathered, later):
    bf16, f32 = jnp.bfloat16, jnp.float32
    anywhere = pl.BlockSpec(memory_space=pl.ANY)
    whole = pl.BlockSpec(memory_space=pltpu.VMEM)
    rows = pl.BlockSpec((B, HEADS * D), lambda j: (j, 0))
    return pl.pallas_call(
        middle_kernel,
        grid=(QB,),
        out_shape=[
            jax.ShapeDtypeStruct((ROWS, HEADS * D), bf16),
            jax.ShapeDtypeStruct((ROWS, HEADS * D), bf16),
            jax.ShapeDtypeStruct((SEQ, B, 2 * D), bf16),
            jax.ShapeDtypeStruct((ROWS + 2 * B, 2 * D), f32),
            jax.ShapeDtypeStruct((B, 2 * D), bf16),
        ],
        in_specs=[pl.BlockSpec(memory_space=pltpu.SMEM), rows, rows, anywhere, anywhere],
        out_specs=[rows, rows, anywhere, whole, whole],
        scratch_shapes=[
            pltpu.VMEM((2, KEYS, 2 * D), bf16),
            pltpu.VMEM((2, KEYS, 2 * D), f32),
            pltpu.VMEM((KEYS, HEADS * B), bf16),
            pltpu.VMEM((KEYS, HEADS * B), bf16),
            pltpu.VMEM((QB + 1, 4, B, 2 * D), bf16),
            pltpu.SemaphoreType.DMA((2, SLOTS)),
            pltpu.SemaphoreType.DMA((QB + 1, 4)),
        ],
        compiler_params=pltpu.CompilerParams(vmem_limit_bytes=VMEM_LIMIT),
        cost_estimate=pl.CostEstimate(
            flops=QB * 6 * 2 * KEYS * HEADS * B * D,
            bytes_accessed=QB * (4 << 20),
            transcendentals=QB * KEYS * HEADS * B,
        ),
    )(info, query_rows, out_grad, gathered, later)


def sum_kernel(
    target, recv_ref, extra_ref, own_ref, edge_ref, edge_core_ref, edge_across_ref, dk_ref, dv_ref, acc
):
    acc[...] = (
        own_ref[:ROWS, :]
        + edge_ref[...]
        + edge_core_ref[0].astype(jnp.float32)
        + edge_across_ref[...].astype(jnp.float32)
    )

    def add(s, carry):
        t = target[s]

        @pl.when(t >= 0)
        def _():
            rows = pl.ds(pl.multiple_of(t * B, B), B)
            acc[rows, :] += recv_ref[s].astype(jnp.float32)

        return carry

    lax.fori_loop(0, SEQ, add, 0)
    t = target[SEQ]

    @pl.when(t >= 0)
    def _():
        rows = pl.ds(pl.multiple_of(t * B, B), B)
        acc[rows, :] += extra_ref[...].astype(jnp.float32)

    dk_ref[...] = acc[:, :D].astype(jnp.bfloat16)
    dv_ref[...] = acc[:, D:].astype(jnp.bfloat16)


def call(kernel, outs, args, scalars=0, later=0, scratch=(), flops=0, bytes_accessed=0, exps=0):
    vmem = pl.BlockSpec(memory_space=pltpu.VMEM)
    smem = pl.BlockSpec(memory_space=pltpu.SMEM)
    return pl.pallas_call(
        kernel,
        out_shape=[jax.ShapeDtypeStruct(shape, dtype) for shape, dtype in outs],
        in_specs=[smem] * scalars
        + [vmem] * (len(args) - scalars - later)
        + [pl.BlockSpec(memory_space=pl.ANY)] * later,
        out_specs=[vmem] * len(outs),
        scratch_shapes=list(scratch),
        compiler_params=pltpu.CompilerParams(vmem_limit_bytes=VMEM_LIMIT),
        cost_estimate=pl.CostEstimate(
            flops=flops, bytes_accessed=bytes_accessed, transcendentals=exps
        ),
    )(*args)


def hold(*values):
    return lax.optimization_barrier(values)


def local(query_rows, key_rows, value_rows, out_grad, random_blocks):
    bf16, f32 = jnp.bfloat16, jnp.float32
    me = lax.axis_index("seq").astype(jnp.int32)
    my_x, my_z, my_c = me >> 4, (me >> 1) & 7, me & 1
    ids = random_blocks.reshape(QB * 3).astype(jnp.int32)

    at_edge = my_z == jnp.where(my_c == 0, EDGE_Z[0], EDGE_Z[1])
    is_root = jnp.logical_or(me == 0, me == SEQ - 1)
    edge_start = my_c * (ROWS - B)

    def edge_half(x):
        return jnp.concatenate(
            [
                lax.dynamic_slice(rows, (edge_start, x * (4 * D)), (B, 4 * D))
                for rows in (query_rows, out_grad)
            ],
            axis=1,
        )

    id_rows = jnp.zeros((PIECE - ROWS, 2 * D), bf16).at[0, : QB * 3].set(ids.astype(bf16))
    mine = jnp.concatenate([jnp.concatenate([key_rows, value_rows], axis=1), id_rows], axis=0)
    partner = permute(mine, ACROSS)
    near = [mine, partner, permute(mine, CORE), permute(partner, CORE)]

    edge = jnp.where(is_root, edge_half(my_x), permute(edge_half(1 - my_x), EDGE_ACROSS))
    edge = jnp.where(at_edge, edge, jnp.zeros_like(edge))
    edge = edge + permute(edge, edge_tree(4))
    both, edge = hold(jnp.concatenate([mine, partner], axis=0), edge)
    gathered = lax.all_gather(both, "seq", axis_index_groups=ZC_GROUPS, tiled=True)
    for step in (2, 1):
        edge = edge + permute(edge, edge_tree(step))

    edge_flops = 2 * 4 * ROWS * ROWS * D
    (stats,) = call(
        edge_stats_kernel,
        [((8, 4 * D), f32)],
        [edge] + near,
        flops=2 * edge_flops,
        bytes_accessed=2 << 20,
        exps=4 * ROWS * ROWS,
    )
    all_stats = lax.all_to_all(
        jnp.broadcast_to(stats, (ZN, *stats.shape)), "seq", 0, 0, axis_index_groups=Z_GROUPS
    )
    edge_oq, edge_own, edge_core, edge_across = call(
        edge_grad_kernel,
        [
            ((B, 8 * D), bf16),
            ((ROWS, 2 * D), f32),
            ((2, ROWS, 2 * D), bf16),
            ((ROWS, 2 * D), f32),
        ],
        [edge] + near + [all_stats],
        flops=6 * edge_flops,
        bytes_accessed=4 << 20,
        exps=4 * ROWS * ROWS,
    )
    edge_core = permute(edge_core, CORE)
    parts = [permute(edge_oq, to_edge(step)) for step in range(1, ZN)]
    edge_across = permute((edge_across + edge_core[1].astype(f32)).astype(bf16), ACROSS)

    info = jnp.concatenate([ids, me[None], jnp.zeros((3,), jnp.int32)])
    attended, query_grad, send, own, extra = middle_call(
        info, query_rows, out_grad, gathered, edge_oq
    )

    *parts, edge_across, send = hold(*parts, edge_across, send)
    oq_here = edge_oq.astype(f32)
    for part in parts:
        oq_here = oq_here + part.astype(f32)
    oq_here = oq_here.astype(bf16)
    oq_other = permute(oq_here, reverse(EDGE_ACROSS))
    extra = permute(extra, [(1, 0), (SEQ - 2, SEQ - 1)])
    recv = lax.all_to_all(send, "seq", 0, 0)

    table = gathered.reshape(SEQ, PIECE, 2 * D)[:, ROWS, : QB * 3].astype(jnp.int32)
    place = jnp.arange(SEQ, dtype=jnp.int32)
    source = (place >> 1) | (((place & 1) ^ my_x) << 4)
    row = source[:, None] * QB + jnp.arange(QB * 3, dtype=jnp.int32)[None, :] // 3
    read = jnp.logical_and(row > 0, row < NB - 1)
    mine_named = jnp.logical_and((table >> 2) == me, read)
    named = jnp.max(jnp.where(mine_named, table & 3, -1), axis=1)
    named = jnp.where(source == me - 1, 0, jnp.where(source == me + 1, QB - 1, named))
    named = jnp.where(me == 0, 0, jnp.where(me == SEQ - 1, QB - 1, named))
    named = jnp.where(source == me, -1, named)
    by_source = jnp.max(
        jnp.where(source[None, :] == place[:, None], named[None, :], -1), axis=1
    )
    extra_at = jnp.where(me == 0, QB - 1, jnp.where(me == SEQ - 1, 0, -1))
    target = jnp.concatenate([by_source, extra_at[None]]).astype(jnp.int32)

    key_grad, value_grad = call(
        sum_kernel,
        [((ROWS, D), bf16), ((ROWS, D), bf16)],
        [target, recv, extra, own, edge_own, edge_core, edge_across],
        scalars=1,
        scratch=[pltpu.VMEM((ROWS, 2 * D), f32)],
        flops=1 << 20,
        bytes_accessed=4 << 20,
    )

    low = jnp.where(my_x == 0, oq_here, oq_other)
    high = jnp.where(my_x == 0, oq_other, oq_here)

    def put(whole, start):
        edge_rows = jnp.concatenate(
            [low[:, start : start + 4 * D], high[:, start : start + 4 * D]], axis=1
        )
        present = lax.dynamic_slice(whole, (edge_start, 0), (B, HEADS * D))
        return lax.dynamic_update_slice(
            whole, jnp.where(is_root, edge_rows, present), (edge_start, 0)
        )

    return put(attended, 0), put(query_grad, 4 * D), key_grad, value_grad


def solution(mesh):
    rows = P("seq", "head")
    return jax.shard_map(
        local,
        mesh=mesh,
        in_specs=(rows, rows, rows, rows, P("seq", None)),
        out_specs=(rows, rows, rows, rows),
        check_vma=False,
    )
```

```python
import functools
import math

import jax
import jax.numpy as jnp
from jax import lax
from jax.experimental import pallas as pl
from jax.experimental.pallas import tpu as pltpu
from jax.sharding import PartitionSpec as P

D = 128
B = 128
SEQ = 32
ZN = 8
QB = 4
NB = SEQ * QB
HEADS = 8
ROWS = QB * B
PIECE = ROWS + 16
SLOTS = 8
KEYS = SLOTS * B
SCALE = 1.0 / math.sqrt(D)
LOG2E = math.log2(math.e)
FAR = -1e30
VMEM_LIMIT = 56 * 1024 * 1024
NT = (((1,), (1,)), ((), ()))
TN = (((0,), (0,)), ((), ()))


def device_of(x, z, c):
    return x * 16 + (z % ZN) * 2 + c


ALL = [(x, z, c) for x in range(2) for z in range(ZN) for c in range(2)]


CORE = [(i, i ^ 1) for i in range(SEQ)]
ACROSS = [(i, i ^ 16) for i in range(SEQ)]
Z_GROUPS = [[device_of(x, z, c) for z in range(ZN)] for x in range(2) for c in range(2)]
ZC_GROUPS = [[device_of(x, z, c) for z in range(ZN) for c in range(2)] for x in range(2)]
EDGE_Z = (0, ZN - 1)
EDGE_ACROSS = [(0, 16), (31, 15)]


def from_edge(step, across):
    return [
        (0, device_of(across, step, 0)),
        (SEQ - 1, device_of(1 - across, ZN - 1 - step, 1)),
    ]


def edge_tree(step):
    pairs = []
    for x in range(2):
        for c, sign in ((0, 1), (1, -1)):
            for r in range(0, ZN, 2 * step):
                ends = [EDGE_Z[c] + sign * r, EDGE_Z[c] + sign * (r + step)]
                pairs.append(tuple(device_of(x, z, c) for z in ends))
    return pairs


def to_edge(step):
    return [
        (device_of(x, EDGE_Z[c] + sign * step, c), device_of(x, EDGE_Z[c], c))
        for x in range(2)
        for c, sign in ((0, 1), (1, -1))
    ]


def reverse(pairs):
    return [(b, a) for a, b in pairs]


def place_of(source, my_x):
    return ((source & 15) << 1) | ((source >> 4) ^ my_x)


def permute(value, pairs):
    return lax.ppermute(value, "seq", pairs)


def dot(a, b, dims=(((1,), (0,)), ((), ()))):
    return lax.dot_general(a, b, dims, preferred_element_type=jnp.float32)


def two_heads(ref_value, first):
    return jnp.concatenate(
        [ref_value[:, first : first + D], ref_value[:, first + D : first + 2 * D]], axis=0
    )


def pack_kernel(ids_ref, k_ref, v_ref, mine_ref):
    mine_ref[:ROWS, :D] = k_ref[...]
    mine_ref[:ROWS, D:] = v_ref[...]
    shape = (PIECE - ROWS, 2 * D)
    column = lax.broadcasted_iota(jnp.int32, shape, 1)
    ids = jnp.zeros(shape, jnp.int32)
    for n in range(QB * 3):
        ids = jnp.where(column == n, ids_ref[n // 3, n % 3], ids)
    mine_ref[ROWS:, :] = ids.astype(jnp.float32).astype(jnp.bfloat16)


def edge_kernel(info, q_ref, g_ref, _, own_ref, other_ref, sems):
    me = info[12]
    start = pl.multiple_of((me & 1) * (ROWS - B), B)
    copies = []
    for side, out in enumerate((own_ref, other_ref)):
        first = pl.multiple_of(((me >> 4) ^ side) * (4 * D), D)
        for n, rows in enumerate((q_ref, g_ref)):
            copies.append(
                pltpu.make_async_copy(
                    rows.at[pl.ds(start, B), pl.ds(first, 4 * D)],
                    out.at[:, pl.ds(n * 4 * D, 4 * D)],
                    sems.at[side, n],
                )
            )
    for copy in copies:
        copy.start()
    for copy in copies:
        copy.wait()


def put_kernel(info, low_ref, high_ref, out_in, dq_in, out_ref, dq_ref, sems):
    me = info[12]
    start = pl.multiple_of((me & 1) * (ROWS - B), B)
    copies = []
    for side, half in enumerate((low_ref, high_ref)):
        for n, rows in enumerate((out_ref, dq_ref)):
            copies.append(
                pltpu.make_async_copy(
                    half.at[:, pl.ds(n * 4 * D, 4 * D)],
                    rows.at[pl.ds(start, B), pl.ds(side * 4 * D, 4 * D)],
                    sems.at[side, n],
                )
            )

    @pl.when(jnp.logical_or(me == 0, me == SEQ - 1))
    def _():
        for copy in copies:
            copy.start()
        for copy in copies:
            copy.wait()


def near_pieces(both_ref, core_ref):
    return [
        (ref[at : at + ROWS, :D], ref[at : at + ROWS, D:])
        for ref in (both_ref, core_ref)
        for at in (0, PIECE)
    ]


def edge_stats_kernel(edge_ref, both_ref, other_ref, stats_ref):
    near = near_pieces(both_ref, other_ref)
    stats_ref[...] = jnp.zeros_like(stats_ref)
    for pair in range(2):
        q2 = two_heads(edge_ref, pair * 2 * D)
        g2 = two_heads(edge_ref, 4 * D + pair * 2 * D)
        scores = [dot(keys, q2, NT) * (SCALE * LOG2E) for keys, _ in near]
        top = scores[0].max(axis=0, keepdims=True)
        for s in scores[1:]:
            top = jnp.maximum(top, s.max(axis=0, keepdims=True))
        total = jnp.zeros_like(top)
        delta = jnp.zeros_like(top)
        for s, (_, values) in zip(scores, near):
            e = jnp.exp2(s - top)
            total = total + e.sum(axis=0, keepdims=True)
            w = dot(values, g2, NT)
            delta = delta + (e * w).sum(axis=0, keepdims=True)
        cols = slice(pair * 2 * D, (pair + 1) * 2 * D)
        stats_ref[0:1, cols] = top
        stats_ref[1:2, cols] = total
        stats_ref[2:3, cols] = delta


def edge_grad_kernel(
    edge_ref, both_ref, other_ref, stats_ref, oq_ref, own_ref, core_ref, across_ref
):
    stats = [stats_ref[n] for n in range(ZN)]
    top = stats[0][0:1]
    for s in stats[1:]:
        top = jnp.maximum(top, s[0:1])
    total = jnp.zeros_like(top)
    delta = jnp.zeros_like(top)
    for s in stats:
        factor = jnp.exp2(s[0:1] - top)
        total = total + s[1:2] * factor
        delta = delta + s[2:3] * factor
    delta = delta / total
    shift = top + jnp.log2(total)
    q_all = jnp.concatenate([two_heads(edge_ref, 0), two_heads(edge_ref, 2 * D)], axis=0)
    g_all = jnp.concatenate([two_heads(edge_ref, 4 * D), two_heads(edge_ref, 6 * D)], axis=0)
    out = None
    for n, (keys, values) in enumerate(near_pieces(both_ref, other_ref)):
        p = jnp.exp2(dot(keys, q_all, NT) * (SCALE * LOG2E) - shift)
        ds = (p * (dot(values, g_all, NT) - delta)).astype(jnp.bfloat16)
        p = p.astype(jnp.bfloat16)
        o = dot(values, p, TN)
        dq = dot(keys, ds, TN)
        out = (o, dq) if out is None else (out[0] + o, out[1] + dq)
        dk = dot(ds, q_all) * SCALE
        dv = dot(p, g_all)
        if n == 0:
            own_ref[:, :D] = dk
            own_ref[:, D:] = dv
        elif n == 1:
            across_ref[:, :D] = dk
            across_ref[:, D:] = dv
        else:
            core_ref[n - 2, :, :D] = dk.astype(jnp.bfloat16)
            core_ref[n - 2, :, D:] = dv.astype(jnp.bfloat16)
    for h in range(4):
        cols = slice(h * D, (h + 1) * D)
        oq_ref[:, cols] = out[0][:, cols].T.astype(jnp.bfloat16)
        oq_ref[:, 4 * D + h * D : 4 * D + (h + 1) * D] = (out[1][:, cols].T * SCALE).astype(
            jnp.bfloat16
        )


def middle_kernel(info, q_ref, g_ref, all_ref, _, *refs):
    out_ref, dq_ref, send_ref, state_ref, side_ref = refs[:5]
    kv, s_ref, e_all, ds_all, slots, sems, slot_sems = refs[5:]
    me = info[12]
    j = pl.program_id(0)
    last_step = j == QB - 1

    def fetch(block, buffer, slot):
        block = jnp.clip(block, 0, NB - 1)
        place = place_of(block >> 2, me >> 4)
        row = pl.multiple_of(place * PIECE + (block & 3) * B, 16)
        return pltpu.make_async_copy(
            all_ref.at[pl.ds(row, B), :], kv.at[buffer, pl.ds(slot * B, B), :], sems.at[buffer, slot]
        )

    def slot_copy(at, which, destination):
        return pltpu.make_async_copy(
            slots.at[at, which], send_ref.at[destination], slot_sems.at[at, which]
        )

    def fetch_all(step, buffer):
        block = me * QB + step
        for slot, name in enumerate((block - 1, block, block + 1, 0, NB - 1)):
            fetch(jnp.int32(name), buffer, slot).start()
        for r in range(3):
            fetch(info[step * 3 + r], buffer, 5 + r).start()

    @pl.when(j == 0)
    def _():
        fetch_all(0, 0)
        state_ref[...] = jnp.zeros_like(state_ref)
        side_ref[...] = jnp.zeros_like(side_ref)

    buffer = j & 1

    @pl.when(jnp.logical_not(last_step))
    def _():
        fetch_all(j + 1, 1 - buffer)

    for slot in range(SLOTS):
        fetch(jnp.int32(0), buffer, slot).wait()

    block = me * QB + j
    middle = jnp.logical_and(block > 0, block < NB - 1)
    to_low = jnp.logical_and(jnp.logical_and(middle, j == 0), me != 1)
    to_high = jnp.logical_and(jnp.logical_and(middle, j == QB - 1), me != SEQ - 2)

    @pl.when(middle)
    def _():
        low_bias = jnp.where(block == 1, FAR, 0.0).astype(jnp.float32)
        high_bias = jnp.where(block == NB - 2, FAR, 0.0).astype(jnp.float32)
        values_t = kv[buffer, :, D:].T
        keys_t = kv[buffer, :, :D].T
        scaled_q, scaled_g = [], []
        pairs = range(HEADS // 2)
        heads = [[slice((2 * p + h) * D, (2 * p + h + 1) * D) for h in range(2)] for p in pairs]
        chunks = [slice(n * B, (n + 1) * B) for n in range(KEYS // B)]

        def scores(pair):
            q_t = jnp.concatenate([q_ref[:, h].T for h in heads[pair]], axis=1)
            top = None
            for n, c in enumerate(chunks):
                s = dot(kv[buffer, c, :D], q_t)
                if n == 0:
                    s = s + low_bias
                if n == 2:
                    s = s + high_bias
                s_ref[pair % 2, c, :] = s
                m = s.max(axis=0, keepdims=True)
                top = m if top is None else jnp.maximum(top, m)
            return top * (SCALE * LOG2E)

        def weights(pair, top):
            cols = slice(pair * 2 * D, (pair + 1) * 2 * D)
            total = None
            for c in chunks:
                e = jnp.exp2(s_ref[pair % 2, c, :] * (SCALE * LOG2E) - top)
                e_all[c, cols] = e.astype(jnp.bfloat16)
                t = e.sum(axis=0, keepdims=True)
                total = t if total is None else total + t
            return 1.0 / total

        def gradients(pair, part):
            cols = slice(pair * 2 * D, (pair + 1) * 2 * D)
            g_t = jnp.concatenate([g_ref[:, h].T for h in heads[pair]], axis=1)
            o = dot(values_t, e_all[:, cols]) * part
            delta = (g_t.astype(jnp.float32) * o).sum(axis=0, keepdims=True)
            for c in chunks:
                e = e_all[c, cols].astype(jnp.float32)
                ds_all[c, cols] = (e * (dot(kv[buffer, c, D:], g_t) - delta)).astype(jnp.bfloat16)
            dq = dot(keys_t, ds_all[:, cols]) * (part * SCALE)
            for n, h in enumerate(heads[pair]):
                one = slice(n * B, (n + 1) * B)
                out_ref[:, h] = o[:, one].T.astype(jnp.bfloat16)
                dq_ref[:, h] = dq[:, one].T.astype(jnp.bfloat16)
                column = part[:, one].T
                scaled_q.append((q_ref[:, h] * (column * SCALE)).astype(jnp.bfloat16))
                scaled_g.append((g_ref[:, h] * column).astype(jnp.bfloat16))

        top = scores(0)
        for pair in pairs:
            part = weights(pair, top)
            if pair + 1 < HEADS // 2:
                top = scores(pair + 1)
            gradients(pair, part)
        dk = dot(ds_all[...], jnp.concatenate(scaled_q, axis=0))
        dv = dot(e_all[...], jnp.concatenate(scaled_g, axis=0))

        def contribution(slot):
            rows = slice(slot * B, (slot + 1) * B)
            return jnp.concatenate([dk[rows], dv[rows]], axis=1)

        def low(slot):
            return contribution(slot).astype(jnp.bfloat16)

        state_ref[pl.ds(pl.multiple_of(j * B, B), B), :] += contribution(1)
        state_ref[ROWS : ROWS + B, :] += contribution(3)
        state_ref[ROWS + B :, :] += contribution(4)

        @pl.when(j > 0)
        def _():
            state_ref[pl.ds(pl.multiple_of((j - 1) * B, B), B), :] += contribution(0)

        @pl.when(j < QB - 1)
        def _():
            state_ref[pl.ds(pl.multiple_of((j + 1) * B, B), B), :] += contribution(2)

        for r in range(3):
            slots[j, r] = low(5 + r)
            slot_copy(j, r, info[j * 3 + r] >> 2).start()

        @pl.when(j == 0)
        def _():
            slots[j, 3] = low(0)

        @pl.when(j == QB - 1)
        def _():
            slots[j, 3] = low(2)

        @pl.when(to_low)
        def _():
            slot_copy(j, 3, me - 1).start()

        @pl.when(to_high)
        def _():
            slot_copy(j, 3, me + 1).start()

        @pl.when(jnp.logical_and(j == 0, me == 1))
        def _():
            side_ref[...] = low(0)

        @pl.when(jnp.logical_and(j == QB - 1, me == SEQ - 2))
        def _():
            side_ref[...] = low(2)

    @pl.when(last_step)
    def _():
        slots[QB, 0] = state_ref[ROWS : ROWS + B, :].astype(jnp.bfloat16)
        slots[QB, 1] = state_ref[ROWS + B :, :].astype(jnp.bfloat16)

        @pl.when(me == 0)
        def _():
            state_ref[:B, :] += state_ref[ROWS : ROWS + B, :]

        @pl.when(me != 0)
        def _():
            slot_copy(QB, 0, 0).start()
            slot_copy(QB, 0, 0).wait()

        @pl.when(me == SEQ - 1)
        def _():
            state_ref[ROWS - B : ROWS, :] += state_ref[ROWS + B :, :]

        @pl.when(me != SEQ - 1)
        def _():
            slot_copy(QB, 1, SEQ - 1).start()
            slot_copy(QB, 1, SEQ - 1).wait()

    @pl.when(middle)
    def _():
        for r in range(3):
            slot_copy(j, r, 0).wait()

    @pl.when(jnp.logical_or(to_low, to_high))
    def _():
        slot_copy(j, 3, 0).wait()


def middle_call(info, query_rows, out_grad, gathered, later):
    bf16, f32 = jnp.bfloat16, jnp.float32
    anywhere = pl.BlockSpec(memory_space=pl.ANY)
    whole = pl.BlockSpec(memory_space=pltpu.VMEM)
    rows = pl.BlockSpec((B, HEADS * D), lambda j: (j, 0))
    return pl.pallas_call(
        middle_kernel,
        grid=(QB,),
        out_shape=[
            jax.ShapeDtypeStruct((ROWS, HEADS * D), bf16),
            jax.ShapeDtypeStruct((ROWS, HEADS * D), bf16),
            jax.ShapeDtypeStruct((SEQ, B, 2 * D), bf16),
            jax.ShapeDtypeStruct((ROWS + 2 * B, 2 * D), f32),
            jax.ShapeDtypeStruct((B, 2 * D), bf16),
        ],
        in_specs=[pl.BlockSpec(memory_space=pltpu.SMEM), rows, rows, anywhere, anywhere],
        out_specs=[rows, rows, anywhere, whole, whole],
        scratch_shapes=[
            pltpu.VMEM((2, KEYS, 2 * D), bf16),
            pltpu.VMEM((2, KEYS, 2 * D), f32),
            pltpu.VMEM((KEYS, HEADS * B), bf16),
            pltpu.VMEM((KEYS, HEADS * B), bf16),
            pltpu.VMEM((QB + 1, 4, B, 2 * D), bf16),
            pltpu.SemaphoreType.DMA((2, SLOTS)),
            pltpu.SemaphoreType.DMA((QB + 1, 4)),
        ],
        compiler_params=pltpu.CompilerParams(vmem_limit_bytes=VMEM_LIMIT),
        cost_estimate=pl.CostEstimate(
            flops=QB * 6 * 2 * KEYS * HEADS * B * D,
            bytes_accessed=QB * (4 << 20),
            transcendentals=QB * KEYS * HEADS * B,
        ),
    )(info, query_rows, out_grad, gathered, later)


def sum_kernel(
    target,
    extra_ref,
    own_ref,
    edge_ref,
    edge_core_ref,
    edge_across_ref,
    recv_ref,
    dk_ref,
    dv_ref,
    acc,
    held,
    sems,
):
    def copy(s):
        return pltpu.make_async_copy(recv_ref.at[s], held.at[s], sems.at[s])

    def begin(s, carry):
        @pl.when(target[s] >= 0)
        def _():
            copy(s).start()

        return carry

    lax.fori_loop(0, SEQ, begin, 0)
    acc[...] = (
        own_ref[:ROWS, :]
        + edge_ref[...]
        + edge_core_ref[0].astype(jnp.float32)
        + edge_across_ref[...].astype(jnp.float32)
    )
    t = target[SEQ]

    @pl.when(t >= 0)
    def _():
        rows = pl.ds(pl.multiple_of(t * B, B), B)
        acc[rows, :] += extra_ref[...].astype(jnp.float32)

    def add(s, carry):
        t = target[s]

        @pl.when(t >= 0)
        def _():
            copy(s).wait()
            rows = pl.ds(pl.multiple_of(t * B, B), B)
            acc[rows, :] += held[s].astype(jnp.float32)

        return carry

    lax.fori_loop(0, SEQ, add, 0)
    dk_ref[...] = acc[:, :D].astype(jnp.bfloat16)
    dv_ref[...] = acc[:, D:].astype(jnp.bfloat16)


def call(kernel, outs, args, scalars=0, later=0, scratch=(), flops=0, bytes_accessed=0, exps=0):
    vmem = pl.BlockSpec(memory_space=pltpu.VMEM)
    smem = pl.BlockSpec(memory_space=pltpu.SMEM)
    return pl.pallas_call(
        kernel,
        out_shape=[jax.ShapeDtypeStruct(shape, dtype) for shape, dtype in outs],
        in_specs=[smem] * scalars
        + [vmem] * (len(args) - scalars - later)
        + [pl.BlockSpec(memory_space=pl.ANY)] * later,
        out_specs=[vmem] * len(outs),
        scratch_shapes=list(scratch),
        compiler_params=pltpu.CompilerParams(vmem_limit_bytes=VMEM_LIMIT),
        cost_estimate=pl.CostEstimate(
            flops=flops, bytes_accessed=bytes_accessed, transcendentals=exps
        ),
    )(*args)


def hold(*values):
    return lax.optimization_barrier(values)


def local(query_rows, key_rows, value_rows, out_grad, random_blocks):
    bf16, f32 = jnp.bfloat16, jnp.float32
    me = lax.axis_index("seq").astype(jnp.int32)
    my_x, my_z, my_c = me >> 4, (me >> 1) & 7, me & 1
    ids = random_blocks.reshape(QB * 3).astype(jnp.int32)

    is_root = jnp.logical_or(me == 0, me == SEQ - 1)
    info = jnp.concatenate([ids, me[None], jnp.zeros((3,), jnp.int32)])
    smem = pl.BlockSpec(memory_space=pltpu.SMEM)
    vmem = pl.BlockSpec(memory_space=pltpu.VMEM)
    anywhere = pl.BlockSpec(memory_space=pl.ANY)
    (mine,) = call(
        pack_kernel,
        [((PIECE, 2 * D), bf16)],
        [random_blocks, key_rows, value_rows],
        scalars=1,
        bytes_accessed=1 << 19,
    )
    partner = permute(mine, ACROSS)
    edge_own, edge_other = pl.pallas_call(
        edge_kernel,
        out_shape=[jax.ShapeDtypeStruct((B, 8 * D), bf16)] * 2,
        in_specs=[smem, anywhere, anywhere, anywhere],
        out_specs=[vmem, vmem],
        scratch_shapes=[pltpu.SemaphoreType.DMA((2, 2))],
        cost_estimate=pl.CostEstimate(flops=0, bytes_accessed=1 << 27, transcendentals=0),
    )(info, query_rows, out_grad, mine)

    edge = jnp.where(is_root, edge_own, jnp.zeros_like(edge_own))
    edge = edge + permute(edge_other, from_edge(0, 1))
    edge = edge + permute(edge_own, from_edge(4, 0))
    edge = edge + permute(edge_other, from_edge(4, 1))
    both, edge = hold(jnp.concatenate([mine, partner], axis=0), edge)
    gathered = lax.all_gather(both, "seq", axis_index_groups=ZC_GROUPS, tiled=True)
    near = [both, permute(both, CORE)]
    for step in (2, 1):
        edge = edge + permute(edge, edge_tree(step))

    edge_flops = 2 * 4 * ROWS * ROWS * D
    (stats,) = call(
        edge_stats_kernel,
        [((8, 4 * D), f32)],
        [edge] + near,
        flops=2 * edge_flops,
        bytes_accessed=2 << 20,
        exps=4 * ROWS * ROWS,
    )
    all_stats = lax.all_to_all(
        jnp.broadcast_to(stats, (ZN, *stats.shape)), "seq", 0, 0, axis_index_groups=Z_GROUPS
    )
    edge_oq, edge_mine, edge_core, edge_across = call(
        edge_grad_kernel,
        [
            ((B, 8 * D), bf16),
            ((ROWS, 2 * D), f32),
            ((2, ROWS, 2 * D), bf16),
            ((ROWS, 2 * D), f32),
        ],
        [edge] + near + [all_stats],
        flops=6 * edge_flops,
        bytes_accessed=4 << 20,
        exps=4 * ROWS * ROWS,
    )
    edge_core = permute(edge_core, CORE)
    oq_sum = edge_oq.astype(f32)
    oq_sum = oq_sum + permute(edge_oq, reverse(edge_tree(1))).astype(f32)
    oq_low = oq_sum.astype(bf16)
    oq_far = [permute(oq_low, to_edge(step)) for step in (4, 6, 2)]
    edge_across = permute((edge_across + edge_core[1].astype(f32)).astype(bf16), ACROSS)

    attended, query_grad, send, own, extra = middle_call(
        info, query_rows, out_grad, gathered, oq_low
    )

    *oq_far, edge_across, send = hold(*oq_far, edge_across, send)
    for part in oq_far:
        oq_sum = oq_sum + part.astype(f32)
    oq_here = oq_sum.astype(bf16)
    oq_other = permute(oq_here, reverse(EDGE_ACROSS))
    extra = permute(extra, [(1, 0), (SEQ - 2, SEQ - 1)])
    recv = lax.all_to_all(send, "seq", 0, 0)

    table = gathered.reshape(SEQ, PIECE, 2 * D)[:, ROWS, : QB * 3].astype(jnp.int32)
    place = jnp.arange(SEQ, dtype=jnp.int32)
    source = (place >> 1) | (((place & 1) ^ my_x) << 4)
    row = source[:, None] * QB + jnp.arange(QB * 3, dtype=jnp.int32)[None, :] // 3
    read = jnp.logical_and(row > 0, row < NB - 1)
    mine_named = jnp.logical_and((table >> 2) == me, read)
    named = jnp.max(jnp.where(mine_named, table & 3, -1), axis=1)
    named = jnp.where(source == me - 1, 0, jnp.where(source == me + 1, QB - 1, named))
    named = jnp.where(me == 0, 0, jnp.where(me == SEQ - 1, QB - 1, named))
    named = jnp.where(source == me, -1, named)
    by_source = jnp.max(
        jnp.where(source[None, :] == place[:, None], named[None, :], -1), axis=1
    )
    extra_at = jnp.where(me == 0, QB - 1, jnp.where(me == SEQ - 1, 0, -1))
    target = jnp.concatenate([by_source, extra_at[None]]).astype(jnp.int32)

    key_grad, value_grad = call(
        sum_kernel,
        [((ROWS, D), bf16), ((ROWS, D), bf16)],
        [target, extra, own, edge_mine, edge_core, edge_across, recv],
        scalars=1,
        later=1,
        scratch=[
            pltpu.VMEM((ROWS, 2 * D), f32),
            pltpu.VMEM((SEQ, B, 2 * D), bf16),
            pltpu.SemaphoreType.DMA((SEQ,)),
        ],
        flops=1 << 20,
        bytes_accessed=4 << 20,
    )

    low = jnp.where(my_x == 0, oq_here, oq_other)
    high = jnp.where(my_x == 0, oq_other, oq_here)

    rows = jax.ShapeDtypeStruct((ROWS, HEADS * D), bf16)
    attended, query_grad = pl.pallas_call(
        put_kernel,
        out_shape=[rows, rows],
        in_specs=[smem, vmem, vmem, anywhere, anywhere],
        out_specs=[anywhere, anywhere],
        input_output_aliases={3: 0, 4: 1},
        scratch_shapes=[pltpu.SemaphoreType.DMA((2, 2))],
        cost_estimate=pl.CostEstimate(flops=0, bytes_accessed=1 << 20, transcendentals=0),
    )(info, low, high, attended, query_grad)
    return attended, query_grad, key_grad, value_grad


def solution(mesh):
    rows = P("seq", "head")
    return jax.shard_map(
        local,
        mesh=mesh,
        in_specs=(rows, rows, rows, rows, P("seq", None)),
        out_specs=(rows, rows, rows, rows),
        check_vma=False,
    )
```

```python
import functools
import math

import jax
import jax.numpy as jnp
from jax import lax
from jax.experimental import pallas as pl
from jax.experimental.pallas import tpu as pltpu
from jax.sharding import PartitionSpec as P

D = 128
B = 128
SEQ = 32
ZN = 8
QB = 4
NB = SEQ * QB
HEADS = 8
ROWS = QB * B
PIECE = ROWS + 16
SLOTS = 8
KEYS = SLOTS * B
SCALE = 1.0 / math.sqrt(D)
LOG2E = math.log2(math.e)
FAR = -1e30
MIB = 1 << 20
NT = (((1,), (1,)), ((), ()))
TN = (((0,), (0,)), ((), ()))


def device_of(x, z, c):
    return x * 16 + (z % ZN) * 2 + c


ALL = [(x, z, c) for x in range(2) for z in range(ZN) for c in range(2)]


CORE = [(i, i ^ 1) for i in range(SEQ)]
ACROSS = [(i, i ^ 16) for i in range(SEQ)]
Z_GROUPS = [[device_of(x, z, c) for z in range(ZN)] for x in range(2) for c in range(2)]
ZC_GROUPS = [[device_of(x, z, c) for z in range(ZN) for c in range(2)] for x in range(2)]
EDGE_Z = (0, ZN - 1)
EDGE_ACROSS = [(0, 16), (31, 15)]


def from_edge(step, across):
    return [
        (0, device_of(across, step, 0)),
        (SEQ - 1, device_of(1 - across, ZN - 1 - step, 1)),
    ]


def edge_tree(step):
    pairs = []
    for x in range(2):
        for c, sign in ((0, 1), (1, -1)):
            for r in range(0, ZN, 2 * step):
                ends = [EDGE_Z[c] + sign * r, EDGE_Z[c] + sign * (r + step)]
                pairs.append(tuple(device_of(x, z, c) for z in ends))
    return pairs


def to_edge(step):
    return [
        (device_of(x, EDGE_Z[c] + sign * step, c), device_of(x, EDGE_Z[c], c))
        for x in range(2)
        for c, sign in ((0, 1), (1, -1))
    ]


def reverse(pairs):
    return [(b, a) for a, b in pairs]


def place_of(source, my_x):
    return ((source & 15) << 1) | ((source >> 4) ^ my_x)


def permute(value, pairs):
    return lax.ppermute(value, "seq", pairs)


def dot(a, b, dims=(((1,), (0,)), ((), ()))):
    return lax.dot_general(a, b, dims, preferred_element_type=jnp.float32)


def two_heads(ref_value, first):
    return jnp.concatenate(
        [ref_value[:, first : first + D], ref_value[:, first + D : first + 2 * D]], axis=0
    )


def pack_kernel(ids_ref, k_ref, v_ref, mine_ref):
    mine_ref[:ROWS, :D] = k_ref[...]
    mine_ref[:ROWS, D:] = v_ref[...]
    shape = (PIECE - ROWS, 2 * D)
    column = lax.broadcasted_iota(jnp.int32, shape, 1)
    ids = jnp.zeros(shape, jnp.int32)
    for n in range(QB * 3):
        ids = jnp.where(column == n, ids_ref[n // 3, n % 3], ids)
    mine_ref[ROWS:, :] = ids.astype(jnp.float32).astype(jnp.bfloat16)


def edge_kernel(info, q_ref, g_ref, _, own_ref, other_ref, sems):
    me = info[12]
    start = pl.multiple_of((me & 1) * (ROWS - B), B)
    copies = []
    for side, out in enumerate((own_ref, other_ref)):
        first = pl.multiple_of(((me >> 4) ^ side) * (4 * D), D)
        for n, rows in enumerate((q_ref, g_ref)):
            copies.append(
                pltpu.make_async_copy(
                    rows.at[pl.ds(start, B), pl.ds(first, 4 * D)],
                    out.at[:, pl.ds(n * 4 * D, 4 * D)],
                    sems.at[side, n],
                )
            )
    for copy in copies:
        copy.start()
    for copy in copies:
        copy.wait()


def put_kernel(info, low_ref, high_ref, out_in, dq_in, out_ref, dq_ref, sems):
    me = info[12]
    start = pl.multiple_of((me & 1) * (ROWS - B), B)
    copies = []
    for side, half in enumerate((low_ref, high_ref)):
        for n, rows in enumerate((out_ref, dq_ref)):
            copies.append(
                pltpu.make_async_copy(
                    half.at[:, pl.ds(n * 4 * D, 4 * D)],
                    rows.at[pl.ds(start, B), pl.ds(side * 4 * D, 4 * D)],
                    sems.at[side, n],
                )
            )

    @pl.when(jnp.logical_or(me == 0, me == SEQ - 1))
    def _():
        for copy in copies:
            copy.start()
        for copy in copies:
            copy.wait()


def near_pieces(both_ref, core_ref):
    return [
        (ref[at : at + ROWS, :D], ref[at : at + ROWS, D:])
        for ref in (both_ref, core_ref)
        for at in (0, PIECE)
    ]


def edge_stats_kernel(edge_ref, both_ref, other_ref, stats_ref):
    near = near_pieces(both_ref, other_ref)
    stats_ref[...] = jnp.zeros_like(stats_ref)
    for pair in range(2):
        q2 = two_heads(edge_ref, pair * 2 * D)
        g2 = two_heads(edge_ref, 4 * D + pair * 2 * D)
        scores = [dot(keys, q2, NT) * (SCALE * LOG2E) for keys, _ in near]
        top = scores[0].max(axis=0, keepdims=True)
        for s in scores[1:]:
            top = jnp.maximum(top, s.max(axis=0, keepdims=True))
        total = jnp.zeros_like(top)
        delta = jnp.zeros_like(top)
        for s, (_, values) in zip(scores, near):
            e = jnp.exp2(s - top)
            total = total + e.sum(axis=0, keepdims=True)
            w = dot(values, g2, NT)
            delta = delta + (e * w).sum(axis=0, keepdims=True)
        cols = slice(pair * 2 * D, (pair + 1) * 2 * D)
        stats_ref[0:1, cols] = top
        stats_ref[1:2, cols] = total
        stats_ref[2:3, cols] = delta


def edge_grad_kernel(
    edge_ref, both_ref, other_ref, stats_ref, oq_ref, own_ref, core_ref, across_ref
):
    stats = [stats_ref[n] for n in range(ZN)]
    top = stats[0][0:1]
    for s in stats[1:]:
        top = jnp.maximum(top, s[0:1])
    total = jnp.zeros_like(top)
    delta = jnp.zeros_like(top)
    for s in stats:
        factor = jnp.exp2(s[0:1] - top)
        total = total + s[1:2] * factor
        delta = delta + s[2:3] * factor
    delta = delta / total
    shift = top + jnp.log2(total)
    q_all = jnp.concatenate([two_heads(edge_ref, 0), two_heads(edge_ref, 2 * D)], axis=0)
    g_all = jnp.concatenate([two_heads(edge_ref, 4 * D), two_heads(edge_ref, 6 * D)], axis=0)
    out = None
    for n, (keys, values) in enumerate(near_pieces(both_ref, other_ref)):
        p = jnp.exp2(dot(keys, q_all, NT) * (SCALE * LOG2E) - shift)
        ds = (p * (dot(values, g_all, NT) - delta)).astype(jnp.bfloat16)
        p = p.astype(jnp.bfloat16)
        o = dot(values, p, TN)
        dq = dot(keys, ds, TN)
        out = (o, dq) if out is None else (out[0] + o, out[1] + dq)
        dk = dot(ds, q_all) * SCALE
        dv = dot(p, g_all)
        if n == 0:
            own_ref[:, :D] = dk
            own_ref[:, D:] = dv
        elif n == 1:
            across_ref[:, :D] = dk
            across_ref[:, D:] = dv
        else:
            core_ref[n - 2, :, :D] = dk.astype(jnp.bfloat16)
            core_ref[n - 2, :, D:] = dv.astype(jnp.bfloat16)
    for h in range(4):
        cols = slice(h * D, (h + 1) * D)
        oq_ref[:, cols] = out[0][:, cols].T.astype(jnp.bfloat16)
        oq_ref[:, 4 * D + h * D : 4 * D + (h + 1) * D] = (out[1][:, cols].T * SCALE).astype(
            jnp.bfloat16
        )


def middle_kernel(info, q_ref, g_ref, all_ref, _, *refs):
    out_ref, dq_ref, send_ref, state_ref, side_ref = refs[:5]
    kv, s_ref, e_all, ds_all, slots, sems, slot_sems = refs[5:]
    me = info[12]
    j = pl.program_id(0)
    last_step = j == QB - 1

    def fetch(block, buffer, slot):
        block = jnp.clip(block, 0, NB - 1)
        place = place_of(block >> 2, me >> 4)
        row = pl.multiple_of(place * PIECE + (block & 3) * B, 16)
        return pltpu.make_async_copy(
            all_ref.at[pl.ds(row, B), :], kv.at[buffer, pl.ds(slot * B, B), :], sems.at[buffer, slot]
        )

    def slot_copy(at, which, destination):
        return pltpu.make_async_copy(
            slots.at[at, which], send_ref.at[destination], slot_sems.at[at, which]
        )

    def fetch_all(step, buffer):
        block = me * QB + step
        for slot, name in enumerate((block - 1, block, block + 1, 0, NB - 1)):
            fetch(jnp.int32(name), buffer, slot).start()
        for r in range(3):
            fetch(info[step * 3 + r], buffer, 5 + r).start()

    @pl.when(j == 0)
    def _():
        fetch_all(0, 0)
        state_ref[...] = jnp.zeros_like(state_ref)
        side_ref[...] = jnp.zeros_like(side_ref)

    buffer = j & 1

    @pl.when(jnp.logical_not(last_step))
    def _():
        fetch_all(j + 1, 1 - buffer)

    for slot in range(SLOTS):
        fetch(jnp.int32(0), buffer, slot).wait()

    block = me * QB + j
    middle = jnp.logical_and(block > 0, block < NB - 1)
    to_low = jnp.logical_and(jnp.logical_and(middle, j == 0), me != 1)
    to_high = jnp.logical_and(jnp.logical_and(middle, j == QB - 1), me != SEQ - 2)

    @pl.when(middle)
    def _():
        low_bias = jnp.where(block == 1, FAR, 0.0).astype(jnp.float32)
        high_bias = jnp.where(block == NB - 2, FAR, 0.0).astype(jnp.float32)
        values_t = kv[buffer, :, D:].T
        keys_t = kv[buffer, :, :D].T
        scaled_q, scaled_g = [], []
        pairs = range(HEADS // 2)
        heads = [[slice((2 * p + h) * D, (2 * p + h + 1) * D) for h in range(2)] for p in pairs]
        chunks = [slice(n * B, (n + 1) * B) for n in range(KEYS // B)]

        def scores(pair):
            q_t = jnp.concatenate([q_ref[:, h].T for h in heads[pair]], axis=1)
            top = None
            for n, c in enumerate(chunks):
                s = dot(kv[buffer, c, :D], q_t)
                if n == 0:
                    s = s + low_bias
                if n == 2:
                    s = s + high_bias
                s_ref[pair % 2, c, :] = s
                m = s.max(axis=0, keepdims=True)
                top = m if top is None else jnp.maximum(top, m)
            return top * (SCALE * LOG2E)

        def weights(pair, top):
            cols = slice(pair * 2 * D, (pair + 1) * 2 * D)
            total = None
            for c in chunks:
                e = jnp.exp2(s_ref[pair % 2, c, :] * (SCALE * LOG2E) - top)
                e_all[c, cols] = e.astype(jnp.bfloat16)
                t = e.sum(axis=0, keepdims=True)
                total = t if total is None else total + t
            return 1.0 / total

        def gradients(pair, part):
            cols = slice(pair * 2 * D, (pair + 1) * 2 * D)
            g_t = jnp.concatenate([g_ref[:, h].T for h in heads[pair]], axis=1)
            o = dot(values_t, e_all[:, cols]) * part
            delta = (g_t.astype(jnp.float32) * o).sum(axis=0, keepdims=True)
            for c in chunks:
                e = e_all[c, cols].astype(jnp.float32)
                ds_all[c, cols] = (e * (dot(kv[buffer, c, D:], g_t) - delta)).astype(jnp.bfloat16)
            dq = dot(keys_t, ds_all[:, cols]) * (part * SCALE)
            for n, h in enumerate(heads[pair]):
                one = slice(n * B, (n + 1) * B)
                out_ref[:, h] = o[:, one].T.astype(jnp.bfloat16)
                dq_ref[:, h] = dq[:, one].T.astype(jnp.bfloat16)
                column = part[:, one].T
                scaled_q.append((q_ref[:, h] * (column * SCALE)).astype(jnp.bfloat16))
                scaled_g.append((g_ref[:, h] * column).astype(jnp.bfloat16))

        top = scores(0)
        for pair in pairs:
            part = weights(pair, top)
            if pair + 1 < HEADS // 2:
                top = scores(pair + 1)
            gradients(pair, part)
        dk = dot(ds_all[...], jnp.concatenate(scaled_q, axis=0))
        dv = dot(e_all[...], jnp.concatenate(scaled_g, axis=0))

        def contribution(slot):
            rows = slice(slot * B, (slot + 1) * B)
            return jnp.concatenate([dk[rows], dv[rows]], axis=1)

        def low(slot):
            return contribution(slot).astype(jnp.bfloat16)

        state_ref[pl.ds(pl.multiple_of(j * B, B), B), :] += contribution(1)
        state_ref[ROWS : ROWS + B, :] += contribution(3)
        state_ref[ROWS + B :, :] += contribution(4)

        @pl.when(j > 0)
        def _():
            state_ref[pl.ds(pl.multiple_of((j - 1) * B, B), B), :] += contribution(0)

        @pl.when(j < QB - 1)
        def _():
            state_ref[pl.ds(pl.multiple_of((j + 1) * B, B), B), :] += contribution(2)

        for r in range(3):
            slots[j, r] = low(5 + r)
            slot_copy(j, r, info[j * 3 + r] >> 2).start()

        @pl.when(j == 0)
        def _():
            slots[j, 3] = low(0)

        @pl.when(j == QB - 1)
        def _():
            slots[j, 3] = low(2)

        @pl.when(to_low)
        def _():
            slot_copy(j, 3, me - 1).start()

        @pl.when(to_high)
        def _():
            slot_copy(j, 3, me + 1).start()

        @pl.when(jnp.logical_and(j == 0, me == 1))
        def _():
            side_ref[...] = low(0)

        @pl.when(jnp.logical_and(j == QB - 1, me == SEQ - 2))
        def _():
            side_ref[...] = low(2)

    @pl.when(last_step)
    def _():
        slots[QB, 0] = state_ref[ROWS : ROWS + B, :].astype(jnp.bfloat16)
        slots[QB, 1] = state_ref[ROWS + B :, :].astype(jnp.bfloat16)

        @pl.when(me == 0)
        def _():
            state_ref[:B, :] += state_ref[ROWS : ROWS + B, :]

        @pl.when(me != 0)
        def _():
            slot_copy(QB, 0, 0).start()
            slot_copy(QB, 0, 0).wait()

        @pl.when(me == SEQ - 1)
        def _():
            state_ref[ROWS - B : ROWS, :] += state_ref[ROWS + B :, :]

        @pl.when(me != SEQ - 1)
        def _():
            slot_copy(QB, 1, SEQ - 1).start()
            slot_copy(QB, 1, SEQ - 1).wait()

    @pl.when(middle)
    def _():
        for r in range(3):
            slot_copy(j, r, 0).wait()

    @pl.when(jnp.logical_or(to_low, to_high))
    def _():
        slot_copy(j, 3, 0).wait()


def middle_call(info, query_rows, out_grad, gathered, later):
    bf16, f32 = jnp.bfloat16, jnp.float32
    anywhere = pl.BlockSpec(memory_space=pl.ANY)
    whole = pl.BlockSpec(memory_space=pltpu.VMEM)
    rows = pl.BlockSpec((B, HEADS * D), lambda j: (j, 0))
    return pl.pallas_call(
        middle_kernel,
        grid=(QB,),
        out_shape=[
            jax.ShapeDtypeStruct((ROWS, HEADS * D), bf16),
            jax.ShapeDtypeStruct((ROWS, HEADS * D), bf16),
            jax.ShapeDtypeStruct((SEQ, B, 2 * D), bf16),
            jax.ShapeDtypeStruct((ROWS + 2 * B, 2 * D), f32),
            jax.ShapeDtypeStruct((B, 2 * D), bf16),
        ],
        in_specs=[pl.BlockSpec(memory_space=pltpu.SMEM), rows, rows, anywhere, anywhere],
        out_specs=[rows, rows, anywhere, whole, whole],
        scratch_shapes=[
            pltpu.VMEM((2, KEYS, 2 * D), bf16),
            pltpu.VMEM((2, KEYS, 2 * D), f32),
            pltpu.VMEM((KEYS, HEADS * B), bf16),
            pltpu.VMEM((KEYS, HEADS * B), bf16),
            pltpu.VMEM((QB + 1, 4, B, 2 * D), bf16),
            pltpu.SemaphoreType.DMA((2, SLOTS)),
            pltpu.SemaphoreType.DMA((QB + 1, 4)),
        ],
        compiler_params=pltpu.CompilerParams(vmem_limit_bytes=56 * MIB),
        cost_estimate=pl.CostEstimate(
            flops=QB * 6 * 2 * KEYS * HEADS * B * D,
            bytes_accessed=QB * (4 << 20),
            transcendentals=QB * KEYS * HEADS * B,
        ),
    )(info, query_rows, out_grad, gathered, later)


def sum_kernel(target, extra_ref, base_ref, recv_ref, dk_ref, dv_ref, acc):
    acc[...] = base_ref[...]
    t = target[SEQ]

    @pl.when(t >= 0)
    def _():
        rows = pl.ds(pl.multiple_of(t * B, B), B)
        acc[rows, :] += extra_ref[...].astype(jnp.float32)

    def add(s, carry):
        t = target[s]

        @pl.when(t >= 0)
        def _():
            rows = pl.ds(pl.multiple_of(t * B, B), B)
            acc[rows, :] += recv_ref[s].astype(jnp.float32)

        return carry

    lax.fori_loop(0, SEQ, add, 0)
    dk_ref[...] = acc[:, :D].astype(jnp.bfloat16)
    dv_ref[...] = acc[:, D:].astype(jnp.bfloat16)


def call(
    kernel, outs, args, vmem_mib, scalars=0, later=0, scratch=(), flops=0, bytes_accessed=0, exps=0
):
    vmem = pl.BlockSpec(memory_space=pltpu.VMEM)
    smem = pl.BlockSpec(memory_space=pltpu.SMEM)
    return pl.pallas_call(
        kernel,
        out_shape=[jax.ShapeDtypeStruct(shape, dtype) for shape, dtype in outs],
        in_specs=[smem] * scalars
        + [vmem] * (len(args) - scalars - later)
        + [pl.BlockSpec(memory_space=pl.ANY)] * later,
        out_specs=[vmem] * len(outs),
        scratch_shapes=list(scratch),
        compiler_params=pltpu.CompilerParams(vmem_limit_bytes=vmem_mib * MIB),
        cost_estimate=pl.CostEstimate(
            flops=flops, bytes_accessed=bytes_accessed, transcendentals=exps
        ),
    )(*args)


def hold(*values):
    return lax.optimization_barrier(values)


def local(query_rows, key_rows, value_rows, out_grad, random_blocks):
    bf16, f32 = jnp.bfloat16, jnp.float32
    me = lax.axis_index("seq").astype(jnp.int32)
    my_x, my_z, my_c = me >> 4, (me >> 1) & 7, me & 1
    ids = random_blocks.reshape(QB * 3).astype(jnp.int32)

    is_root = jnp.logical_or(me == 0, me == SEQ - 1)
    info = jnp.concatenate([ids, me[None], jnp.zeros((3,), jnp.int32)])
    smem = pl.BlockSpec(memory_space=pltpu.SMEM)
    vmem = pl.BlockSpec(memory_space=pltpu.VMEM)
    anywhere = pl.BlockSpec(memory_space=pl.ANY)
    (mine,) = call(
        pack_kernel,
        [((PIECE, 2 * D), bf16)],
        [random_blocks, key_rows, value_rows],
        56,
        scalars=1,
        bytes_accessed=1 << 19,
    )
    partner = permute(mine, ACROSS)
    edge_own, edge_other = pl.pallas_call(
        edge_kernel,
        out_shape=[jax.ShapeDtypeStruct((B, 8 * D), bf16)] * 2,
        in_specs=[smem, anywhere, anywhere, anywhere],
        out_specs=[vmem, vmem],
        scratch_shapes=[pltpu.SemaphoreType.DMA((2, 2))],
        compiler_params=pltpu.CompilerParams(vmem_limit_bytes=56 * MIB),
        cost_estimate=pl.CostEstimate(flops=0, bytes_accessed=1 << 27, transcendentals=0),
    )(info, query_rows, out_grad, mine)

    edge = jnp.where(is_root, edge_own, jnp.zeros_like(edge_own))
    edge = edge + permute(edge_other, from_edge(0, 1))
    edge = edge + permute(edge_own, from_edge(4, 0))
    edge = edge + permute(edge_other, from_edge(4, 1))
    both, edge = hold(jnp.concatenate([mine, partner], axis=0), edge)
    gathered = lax.all_gather(both, "seq", axis_index_groups=ZC_GROUPS, tiled=True)
    near = [both, permute(both, CORE)]
    for step in (2, 1):
        edge = edge + permute(edge, edge_tree(step))

    edge_flops = 2 * 4 * ROWS * ROWS * D
    (stats,) = call(
        edge_stats_kernel,
        [((8, 4 * D), f32)],
        [edge] + near,
        24,
        flops=2 * edge_flops,
        bytes_accessed=2 << 20,
        exps=4 * ROWS * ROWS,
    )
    all_stats = lax.all_to_all(
        jnp.broadcast_to(stats, (ZN, *stats.shape)), "seq", 0, 0, axis_index_groups=Z_GROUPS
    )
    edge_oq, edge_mine, edge_core, edge_across = call(
        edge_grad_kernel,
        [
            ((B, 8 * D), bf16),
            ((ROWS, 2 * D), f32),
            ((2, ROWS, 2 * D), bf16),
            ((ROWS, 2 * D), f32),
        ],
        [edge] + near + [all_stats],
        24,
        flops=6 * edge_flops,
        bytes_accessed=4 << 20,
        exps=4 * ROWS * ROWS,
    )
    edge_core = permute(edge_core, CORE)
    oq_sum = edge_oq.astype(f32)
    oq_sum = oq_sum + permute(edge_oq, reverse(edge_tree(1))).astype(f32)
    oq_low = oq_sum.astype(bf16)
    oq_far = [permute(oq_low, to_edge(step)) for step in (4, 6, 2)]
    edge_across = permute((edge_across + edge_core[1].astype(f32)).astype(bf16), ACROSS)

    attended, query_grad, send, own, extra = middle_call(
        info, query_rows, out_grad, gathered, oq_low
    )

    *oq_far, edge_across, send = hold(*oq_far, edge_across, send)
    for part in oq_far:
        oq_sum = oq_sum + part.astype(f32)
    oq_here = oq_sum.astype(bf16)
    oq_other = permute(oq_here, reverse(EDGE_ACROSS))
    extra = permute(extra, [(1, 0), (SEQ - 2, SEQ - 1)])
    recv = lax.all_to_all(send, "seq", 0, 0)

    table = gathered.reshape(SEQ, PIECE, 2 * D)[:, ROWS, : QB * 3].astype(jnp.int32)
    place = jnp.arange(SEQ, dtype=jnp.int32)
    source = (place >> 1) | (((place & 1) ^ my_x) << 4)
    row = source[:, None] * QB + jnp.arange(QB * 3, dtype=jnp.int32)[None, :] // 3
    read = jnp.logical_and(row > 0, row < NB - 1)
    mine_named = jnp.logical_and((table >> 2) == me, read)
    named = jnp.max(jnp.where(mine_named, table & 3, -1), axis=1)
    named = jnp.where(source == me - 1, 0, jnp.where(source == me + 1, QB - 1, named))
    named = jnp.where(me == 0, 0, jnp.where(me == SEQ - 1, QB - 1, named))
    named = jnp.where(source == me, -1, named)
    by_source = jnp.max(
        jnp.where(source[None, :] == place[:, None], named[None, :], -1), axis=1
    )
    extra_at = jnp.where(me == 0, QB - 1, jnp.where(me == SEQ - 1, 0, -1))
    target = jnp.concatenate([by_source, extra_at[None]]).astype(jnp.int32)

    base = own[:ROWS] + edge_mine + edge_core[0].astype(f32) + edge_across.astype(f32)
    key_grad, value_grad = call(
        sum_kernel,
        [((ROWS, D), bf16), ((ROWS, D), bf16)],
        [target, extra, base, recv],
        12,
        scalars=1,
        scratch=[pltpu.VMEM((ROWS, 2 * D), f32)],
        flops=1 << 20,
        bytes_accessed=4 << 20,
    )

    low = jnp.where(my_x == 0, oq_here, oq_other)
    high = jnp.where(my_x == 0, oq_other, oq_here)

    rows = jax.ShapeDtypeStruct((ROWS, HEADS * D), bf16)
    attended, query_grad = pl.pallas_call(
        put_kernel,
        out_shape=[rows, rows],
        in_specs=[smem, vmem, vmem, anywhere, anywhere],
        out_specs=[anywhere, anywhere],
        input_output_aliases={3: 0, 4: 1},
        scratch_shapes=[pltpu.SemaphoreType.DMA((2, 2))],
        compiler_params=pltpu.CompilerParams(vmem_limit_bytes=8 * MIB),
        cost_estimate=pl.CostEstimate(flops=0, bytes_accessed=1 << 20, transcendentals=0),
    )(info, low, high, attended, query_grad)
    return attended, query_grad, key_grad, value_grad


def solution(mesh):
    rows = P("seq", "head")
    return jax.shard_map(
        local,
        mesh=mesh,
        in_specs=(rows, rows, rows, rows, P("seq", None)),
        out_specs=(rows, rows, rows, rows),
        check_vma=False,
    )
```

```python
import functools
import math

import jax
import jax.numpy as jnp
from jax import lax
from jax.experimental import pallas as pl
from jax.experimental.pallas import tpu as pltpu
from jax.sharding import PartitionSpec as P

D = 128
B = 128
SEQ = 32
ZN = 8
QB = 4
NB = SEQ * QB
HEADS = 8
ROWS = QB * B
PIECE = ROWS + 16
SLOTS = 8
KEYS = SLOTS * B
SCALE = 1.0 / math.sqrt(D)
LOG2E = math.log2(math.e)
FAR = -1e30
MIB = 1 << 20
NT = (((1,), (1,)), ((), ()))
TN = (((0,), (0,)), ((), ()))


def device_of(x, z, c):
    return x * 16 + (z % ZN) * 2 + c


ALL = [(x, z, c) for x in range(2) for z in range(ZN) for c in range(2)]


CORE = [(i, i ^ 1) for i in range(SEQ)]
ACROSS = [(i, i ^ 16) for i in range(SEQ)]
Z_GROUPS = [[device_of(x, z, c) for z in range(ZN)] for x in range(2) for c in range(2)]
ZC_GROUPS = [[device_of(x, z, c) for z in range(ZN) for c in range(2)] for x in range(2)]
EDGE_Z = (0, ZN - 1)
EDGE_ACROSS = [(0, 16), (31, 15)]


def from_edge(step, across):
    return [
        (0, device_of(across, step, 0)),
        (SEQ - 1, device_of(1 - across, ZN - 1 - step, 1)),
    ]


def edge_tree(step):
    pairs = []
    for x in range(2):
        for c, sign in ((0, 1), (1, -1)):
            for r in range(0, ZN, 2 * step):
                ends = [EDGE_Z[c] + sign * r, EDGE_Z[c] + sign * (r + step)]
                pairs.append(tuple(device_of(x, z, c) for z in ends))
    return pairs


def to_edge(step):
    return [
        (device_of(x, EDGE_Z[c] + sign * step, c), device_of(x, EDGE_Z[c], c))
        for x in range(2)
        for c, sign in ((0, 1), (1, -1))
    ]


def reverse(pairs):
    return [(b, a) for a, b in pairs]


def place_of(source, my_x):
    return ((source & 15) << 1) | ((source >> 4) ^ my_x)


def permute(value, pairs):
    return lax.ppermute(value, "seq", pairs)


def dot(a, b, dims=(((1,), (0,)), ((), ()))):
    return lax.dot_general(a, b, dims, preferred_element_type=jnp.float32)


def two_heads(ref_value, first):
    return jnp.concatenate(
        [ref_value[:, first : first + D], ref_value[:, first + D : first + 2 * D]], axis=0
    )


def pack_kernel(ids_ref, k_ref, v_ref, q_ref, g_ref, mine_ref, own_ref, other_ref, sems):
    me = lax.axis_index("seq")
    start = pl.multiple_of((me & 1) * (ROWS - B), B)
    copies = []
    for side, out in enumerate((own_ref, other_ref)):
        first = pl.multiple_of(((me >> 4) ^ side) * (4 * D), D)
        for n, rows in enumerate((q_ref, g_ref)):
            copies.append(
                pltpu.make_async_copy(
                    rows.at[pl.ds(start, B), pl.ds(first, 4 * D)],
                    out.at[:, pl.ds(n * 4 * D, 4 * D)],
                    sems.at[side, n],
                )
            )
    for copy in copies:
        copy.start()
    mine_ref[:ROWS, :D] = k_ref[...]
    mine_ref[:ROWS, D:] = v_ref[...]
    shape = (PIECE - ROWS, 2 * D)
    column = lax.broadcasted_iota(jnp.int32, shape, 1)
    ids = jnp.zeros(shape, jnp.int32)
    for n in range(QB * 3):
        ids = jnp.where(column == n, ids_ref[n // 3, n % 3], ids)
    mine_ref[ROWS:, :] = ids.astype(jnp.float32).astype(jnp.bfloat16)
    for copy in copies:
        copy.wait()


def put_kernel(info, low_ref, high_ref, out_in, dq_in, out_ref, dq_ref, sems):
    me = info[12]
    start = pl.multiple_of((me & 1) * (ROWS - B), B)
    copies = []
    for side, half in enumerate((low_ref, high_ref)):
        for n, rows in enumerate((out_ref, dq_ref)):
            copies.append(
                pltpu.make_async_copy(
                    half.at[:, pl.ds(n * 4 * D, 4 * D)],
                    rows.at[pl.ds(start, B), pl.ds(side * 4 * D, 4 * D)],
                    sems.at[side, n],
                )
            )

    @pl.when(jnp.logical_or(me == 0, me == SEQ - 1))
    def _():
        for copy in copies:
            copy.start()
        for copy in copies:
            copy.wait()


def near_pieces(both_ref, core_ref):
    return [
        (ref[at : at + ROWS, :D], ref[at : at + ROWS, D:])
        for ref in (both_ref, core_ref)
        for at in (0, PIECE)
    ]


def edge_stats_kernel(edge_ref, both_ref, other_ref, stats_ref):
    near = near_pieces(both_ref, other_ref)
    stats_ref[...] = jnp.zeros_like(stats_ref)
    for pair in range(2):
        q2 = two_heads(edge_ref, pair * 2 * D)
        g2 = two_heads(edge_ref, 4 * D + pair * 2 * D)
        scores = [dot(keys, q2, NT) * (SCALE * LOG2E) for keys, _ in near]
        top = scores[0].max(axis=0, keepdims=True)
        for s in scores[1:]:
            top = jnp.maximum(top, s.max(axis=0, keepdims=True))
        total = jnp.zeros_like(top)
        delta = jnp.zeros_like(top)
        for s, (_, values) in zip(scores, near):
            e = jnp.exp2(s - top)
            total = total + e.sum(axis=0, keepdims=True)
            w = dot(values, g2, NT)
            delta = delta + (e * w).sum(axis=0, keepdims=True)
        cols = slice(pair * 2 * D, (pair + 1) * 2 * D)
        stats_ref[0:1, cols] = top
        stats_ref[1:2, cols] = total
        stats_ref[2:3, cols] = delta


def edge_grad_kernel(
    edge_ref, both_ref, other_ref, stats_ref, oq_ref, own_ref, core_ref, across_ref
):
    stats = [stats_ref[n] for n in range(ZN)]
    top = stats[0][0:1]
    for s in stats[1:]:
        top = jnp.maximum(top, s[0:1])
    total = jnp.zeros_like(top)
    delta = jnp.zeros_like(top)
    for s in stats:
        factor = jnp.exp2(s[0:1] - top)
        total = total + s[1:2] * factor
        delta = delta + s[2:3] * factor
    delta = delta / total
    shift = top + jnp.log2(total)
    q_all = jnp.concatenate([two_heads(edge_ref, 0), two_heads(edge_ref, 2 * D)], axis=0)
    g_all = jnp.concatenate([two_heads(edge_ref, 4 * D), two_heads(edge_ref, 6 * D)], axis=0)
    out = None
    for n, (keys, values) in enumerate(near_pieces(both_ref, other_ref)):
        p = jnp.exp2(dot(keys, q_all, NT) * (SCALE * LOG2E) - shift)
        ds = (p * (dot(values, g_all, NT) - delta)).astype(jnp.bfloat16)
        p = p.astype(jnp.bfloat16)
        o = dot(values, p, TN)
        dq = dot(keys, ds, TN)
        out = (o, dq) if out is None else (out[0] + o, out[1] + dq)
        dk = dot(ds, q_all) * SCALE
        dv = dot(p, g_all)
        if n == 0:
            own_ref[:, :D] = dk
            own_ref[:, D:] = dv
        elif n == 1:
            across_ref[:, :D] = dk
            across_ref[:, D:] = dv
        else:
            core_ref[n - 2, :, :D] = dk.astype(jnp.bfloat16)
            core_ref[n - 2, :, D:] = dv.astype(jnp.bfloat16)
    for h in range(4):
        cols = slice(h * D, (h + 1) * D)
        oq_ref[:, cols] = out[0][:, cols].T.astype(jnp.bfloat16)
        oq_ref[:, 4 * D + h * D : 4 * D + (h + 1) * D] = (out[1][:, cols].T * SCALE).astype(
            jnp.bfloat16
        )


def middle_kernel(info, q_ref, g_ref, all_ref, _, *refs):
    out_ref, dq_ref, send_ref, state_ref, side_ref = refs[:5]
    kv, s_ref, e_all, ds_all, slots, sems, slot_sems = refs[5:]
    me = info[12]
    j = pl.program_id(0)
    last_step = j == QB - 1

    def fetch(block, buffer, slot):
        block = jnp.clip(block, 0, NB - 1)
        place = place_of(block >> 2, me >> 4)
        row = pl.multiple_of(place * PIECE + (block & 3) * B, 16)
        return pltpu.make_async_copy(
            all_ref.at[pl.ds(row, B), :], kv.at[buffer, pl.ds(slot * B, B), :], sems.at[buffer, slot]
        )

    def slot_copy(at, which, destination):
        return pltpu.make_async_copy(
            slots.at[at, which], send_ref.at[destination], slot_sems.at[at, which]
        )

    def fetch_all(step, buffer):
        block = me * QB + step
        for slot, name in enumerate((block - 1, block, block + 1, 0, NB - 1)):
            fetch(jnp.int32(name), buffer, slot).start()
        for r in range(3):
            fetch(info[step * 3 + r], buffer, 5 + r).start()

    @pl.when(j == 0)
    def _():
        fetch_all(0, 0)
        state_ref[...] = jnp.zeros_like(state_ref)
        side_ref[...] = jnp.zeros_like(side_ref)

    buffer = j & 1

    @pl.when(jnp.logical_not(last_step))
    def _():
        fetch_all(j + 1, 1 - buffer)

    for slot in range(SLOTS):
        fetch(jnp.int32(0), buffer, slot).wait()

    block = me * QB + j
    middle = jnp.logical_and(block > 0, block < NB - 1)
    to_low = jnp.logical_and(jnp.logical_and(middle, j == 0), me != 1)
    to_high = jnp.logical_and(jnp.logical_and(middle, j == QB - 1), me != SEQ - 2)

    @pl.when(middle)
    def _():
        low_bias = jnp.where(block == 1, FAR, 0.0).astype(jnp.float32)
        high_bias = jnp.where(block == NB - 2, FAR, 0.0).astype(jnp.float32)
        values_t = kv[buffer, :, D:].T
        keys_t = kv[buffer, :, :D].T
        scaled_q, scaled_g = [], []
        pairs = range(HEADS // 2)
        heads = [[slice((2 * p + h) * D, (2 * p + h + 1) * D) for h in range(2)] for p in pairs]
        chunks = [slice(n * B, (n + 1) * B) for n in range(KEYS // B)]

        def scores(pair):
            q_t = jnp.concatenate([q_ref[:, h].T for h in heads[pair]], axis=1)
            top = None
            for n, c in enumerate(chunks):
                s = dot(kv[buffer, c, :D], q_t)
                if n == 0:
                    s = s + low_bias
                if n == 2:
                    s = s + high_bias
                s_ref[pair % 2, c, :] = s
                m = s.max(axis=0, keepdims=True)
                top = m if top is None else jnp.maximum(top, m)
            return top * (SCALE * LOG2E)

        def weights(pair, top):
            cols = slice(pair * 2 * D, (pair + 1) * 2 * D)
            total = None
            for c in chunks:
                e = jnp.exp2(s_ref[pair % 2, c, :] * (SCALE * LOG2E) - top)
                e_all[c, cols] = e.astype(jnp.bfloat16)
                t = e.sum(axis=0, keepdims=True)
                total = t if total is None else total + t
            return 1.0 / total

        def gradients(pair, part):
            cols = slice(pair * 2 * D, (pair + 1) * 2 * D)
            g_t = jnp.concatenate([g_ref[:, h].T for h in heads[pair]], axis=1)
            o = dot(values_t, e_all[:, cols]) * part
            delta = (g_t.astype(jnp.float32) * o).sum(axis=0, keepdims=True)
            for c in chunks:
                e = e_all[c, cols].astype(jnp.float32)
                ds_all[c, cols] = (e * (dot(kv[buffer, c, D:], g_t) - delta)).astype(jnp.bfloat16)
            dq = dot(keys_t, ds_all[:, cols]) * (part * SCALE)
            for n, h in enumerate(heads[pair]):
                one = slice(n * B, (n + 1) * B)
                out_ref[:, h] = o[:, one].T.astype(jnp.bfloat16)
                dq_ref[:, h] = dq[:, one].T.astype(jnp.bfloat16)
                column = part[:, one].T
                scaled_q.append((q_ref[:, h] * (column * SCALE)).astype(jnp.bfloat16))
                scaled_g.append((g_ref[:, h] * column).astype(jnp.bfloat16))

        top = scores(0)
        for pair in pairs:
            part = weights(pair, top)
            if pair + 1 < HEADS // 2:
                top = scores(pair + 1)
            gradients(pair, part)
        dk = dot(ds_all[...], jnp.concatenate(scaled_q, axis=0))
        dv = dot(e_all[...], jnp.concatenate(scaled_g, axis=0))

        def contribution(slot):
            rows = slice(slot * B, (slot + 1) * B)
            return jnp.concatenate([dk[rows], dv[rows]], axis=1)

        def low(slot):
            return contribution(slot).astype(jnp.bfloat16)

        state_ref[pl.ds(pl.multiple_of(j * B, B), B), :] += contribution(1)
        state_ref[ROWS : ROWS + B, :] += contribution(3)
        state_ref[ROWS + B :, :] += contribution(4)

        @pl.when(j > 0)
        def _():
            state_ref[pl.ds(pl.multiple_of((j - 1) * B, B), B), :] += contribution(0)

        @pl.when(j < QB - 1)
        def _():
            state_ref[pl.ds(pl.multiple_of((j + 1) * B, B), B), :] += contribution(2)

        for r in range(3):
            slots[j, r] = low(5 + r)
            slot_copy(j, r, info[j * 3 + r] >> 2).start()

        @pl.when(j == 0)
        def _():
            slots[j, 3] = low(0)

        @pl.when(j == QB - 1)
        def _():
            slots[j, 3] = low(2)

        @pl.when(to_low)
        def _():
            slot_copy(j, 3, me - 1).start()

        @pl.when(to_high)
        def _():
            slot_copy(j, 3, me + 1).start()

        @pl.when(jnp.logical_and(j == 0, me == 1))
        def _():
            side_ref[...] = low(0)

        @pl.when(jnp.logical_and(j == QB - 1, me == SEQ - 2))
        def _():
            side_ref[...] = low(2)

    @pl.when(last_step)
    def _():
        slots[QB, 0] = state_ref[ROWS : ROWS + B, :].astype(jnp.bfloat16)
        slots[QB, 1] = state_ref[ROWS + B :, :].astype(jnp.bfloat16)

        @pl.when(me == 0)
        def _():
            state_ref[:B, :] += state_ref[ROWS : ROWS + B, :]

        @pl.when(me != 0)
        def _():
            slot_copy(QB, 0, 0).start()
            slot_copy(QB, 0, 0).wait()

        @pl.when(me == SEQ - 1)
        def _():
            state_ref[ROWS - B : ROWS, :] += state_ref[ROWS + B :, :]

        @pl.when(me != SEQ - 1)
        def _():
            slot_copy(QB, 1, SEQ - 1).start()
            slot_copy(QB, 1, SEQ - 1).wait()

    @pl.when(middle)
    def _():
        for r in range(3):
            slot_copy(j, r, 0).wait()

    @pl.when(jnp.logical_or(to_low, to_high))
    def _():
        slot_copy(j, 3, 0).wait()


def middle_call(info, query_rows, out_grad, gathered, later):
    bf16, f32 = jnp.bfloat16, jnp.float32
    anywhere = pl.BlockSpec(memory_space=pl.ANY)
    whole = pl.BlockSpec(memory_space=pltpu.VMEM)
    rows = pl.BlockSpec((B, HEADS * D), lambda j: (j, 0))
    return pl.pallas_call(
        middle_kernel,
        grid=(QB,),
        out_shape=[
            jax.ShapeDtypeStruct((ROWS, HEADS * D), bf16),
            jax.ShapeDtypeStruct((ROWS, HEADS * D), bf16),
            jax.ShapeDtypeStruct((SEQ, B, 2 * D), bf16),
            jax.ShapeDtypeStruct((ROWS + 2 * B, 2 * D), f32),
            jax.ShapeDtypeStruct((B, 2 * D), bf16),
        ],
        in_specs=[pl.BlockSpec(memory_space=pltpu.SMEM), rows, rows, anywhere, anywhere],
        out_specs=[rows, rows, anywhere, whole, whole],
        scratch_shapes=[
            pltpu.VMEM((2, KEYS, 2 * D), bf16),
            pltpu.VMEM((2, KEYS, 2 * D), f32),
            pltpu.VMEM((KEYS, HEADS * B), bf16),
            pltpu.VMEM((KEYS, HEADS * B), bf16),
            pltpu.VMEM((QB + 1, 4, B, 2 * D), bf16),
            pltpu.SemaphoreType.DMA((2, SLOTS)),
            pltpu.SemaphoreType.DMA((QB + 1, 4)),
        ],
        compiler_params=pltpu.CompilerParams(vmem_limit_bytes=56 * MIB),
        cost_estimate=pl.CostEstimate(
            flops=QB * 6 * 2 * KEYS * HEADS * B * D,
            bytes_accessed=QB * (4 << 20),
            transcendentals=QB * KEYS * HEADS * B,
        ),
    )(info, query_rows, out_grad, gathered, later)


def sum_kernel(target, extra_ref, base_ref, recv_ref, dk_ref, dv_ref, acc):
    acc[...] = base_ref[...]
    t = target[SEQ]

    @pl.when(t >= 0)
    def _():
        rows = pl.ds(pl.multiple_of(t * B, B), B)
        acc[rows, :] += extra_ref[...].astype(jnp.float32)

    def add(s, carry):
        t = target[s]

        @pl.when(t >= 0)
        def _():
            rows = pl.ds(pl.multiple_of(t * B, B), B)
            acc[rows, :] += recv_ref[s].astype(jnp.float32)

        return carry

    lax.fori_loop(0, SEQ, add, 0)
    dk_ref[...] = acc[:, :D].astype(jnp.bfloat16)
    dv_ref[...] = acc[:, D:].astype(jnp.bfloat16)


def call(
    kernel, outs, args, vmem_mib, scalars=0, later=0, scratch=(), flops=0, bytes_accessed=0, exps=0
):
    vmem = pl.BlockSpec(memory_space=pltpu.VMEM)
    smem = pl.BlockSpec(memory_space=pltpu.SMEM)
    return pl.pallas_call(
        kernel,
        out_shape=[jax.ShapeDtypeStruct(shape, dtype) for shape, dtype in outs],
        in_specs=[smem] * scalars
        + [vmem] * (len(args) - scalars - later)
        + [pl.BlockSpec(memory_space=pl.ANY)] * later,
        out_specs=[vmem] * len(outs),
        scratch_shapes=list(scratch),
        compiler_params=pltpu.CompilerParams(vmem_limit_bytes=vmem_mib * MIB),
        cost_estimate=pl.CostEstimate(
            flops=flops, bytes_accessed=bytes_accessed, transcendentals=exps
        ),
    )(*args)


def hold(*values):
    return lax.optimization_barrier(values)


def local(query_rows, key_rows, value_rows, out_grad, random_blocks):
    bf16, f32 = jnp.bfloat16, jnp.float32
    me = lax.axis_index("seq").astype(jnp.int32)
    my_x, my_z, my_c = me >> 4, (me >> 1) & 7, me & 1
    ids = random_blocks.reshape(QB * 3).astype(jnp.int32)

    is_root = jnp.logical_or(me == 0, me == SEQ - 1)
    info = jnp.concatenate([ids, me[None], jnp.zeros((3,), jnp.int32)])
    smem = pl.BlockSpec(memory_space=pltpu.SMEM)
    vmem = pl.BlockSpec(memory_space=pltpu.VMEM)
    anywhere = pl.BlockSpec(memory_space=pl.ANY)
    mine, edge_own, edge_other = pl.pallas_call(
        pack_kernel,
        out_shape=[
            jax.ShapeDtypeStruct((PIECE, 2 * D), bf16),
            jax.ShapeDtypeStruct((B, 8 * D), bf16),
            jax.ShapeDtypeStruct((B, 8 * D), bf16),
        ],
        in_specs=[smem, vmem, vmem, anywhere, anywhere],
        out_specs=[vmem, vmem, vmem],
        scratch_shapes=[pltpu.SemaphoreType.DMA((2, 2))],
        compiler_params=pltpu.CompilerParams(vmem_limit_bytes=56 * MIB),
        cost_estimate=pl.CostEstimate(flops=0, bytes_accessed=2 << 20, transcendentals=0),
    )(random_blocks, key_rows, value_rows, query_rows, out_grad)
    partner = permute(mine, ACROSS)

    edge = jnp.where(is_root, edge_own, jnp.zeros_like(edge_own))
    edge = edge + permute(edge_other, from_edge(0, 1))
    edge = edge + permute(edge_own, from_edge(4, 0))
    edge = edge + permute(edge_other, from_edge(4, 1))
    both, edge = hold(jnp.concatenate([mine, partner], axis=0), edge)
    gathered = lax.all_gather(both, "seq", axis_index_groups=ZC_GROUPS, tiled=True)
    near = [both, permute(both, CORE)]
    for step in (2, 1):
        edge = edge + permute(edge, edge_tree(step))

    edge_flops = 2 * 4 * ROWS * ROWS * D
    (stats,) = call(
        edge_stats_kernel,
        [((8, 4 * D), f32)],
        [edge] + near,
        24,
        flops=2 * edge_flops,
        bytes_accessed=2 << 20,
        exps=4 * ROWS * ROWS,
    )
    all_stats = lax.all_to_all(
        jnp.broadcast_to(stats, (ZN, *stats.shape)), "seq", 0, 0, axis_index_groups=Z_GROUPS
    )
    edge_oq, edge_mine, edge_core, edge_across = call(
        edge_grad_kernel,
        [
            ((B, 8 * D), bf16),
            ((ROWS, 2 * D), f32),
            ((2, ROWS, 2 * D), bf16),
            ((ROWS, 2 * D), f32),
        ],
        [edge] + near + [all_stats],
        24,
        flops=6 * edge_flops,
        bytes_accessed=4 << 20,
        exps=4 * ROWS * ROWS,
    )
    edge_core = permute(edge_core, CORE)
    oq_sum = edge_oq.astype(f32)
    oq_sum = oq_sum + permute(edge_oq, reverse(edge_tree(1))).astype(f32)
    oq_low = oq_sum.astype(bf16)
    oq_far = [permute(oq_low, to_edge(step)) for step in (4, 6, 2)]
    edge_across = permute((edge_across + edge_core[1].astype(f32)).astype(bf16), ACROSS)

    attended, query_grad, send, own, extra = middle_call(
        info, query_rows, out_grad, gathered, oq_low
    )

    *oq_far, edge_across, send = hold(*oq_far, edge_across, send)
    for part in oq_far:
        oq_sum = oq_sum + part.astype(f32)
    oq_here = oq_sum.astype(bf16)
    oq_other = permute(oq_here, reverse(EDGE_ACROSS))
    extra = permute(extra, [(1, 0), (SEQ - 2, SEQ - 1)])
    recv = lax.all_to_all(send, "seq", 0, 0)

    table = gathered.reshape(SEQ, PIECE, 2 * D)[:, ROWS, : QB * 3].astype(jnp.int32)
    place = jnp.arange(SEQ, dtype=jnp.int32)
    source = (place >> 1) | (((place & 1) ^ my_x) << 4)
    row = source[:, None] * QB + jnp.arange(QB * 3, dtype=jnp.int32)[None, :] // 3
    read = jnp.logical_and(row > 0, row < NB - 1)
    mine_named = jnp.logical_and((table >> 2) == me, read)
    named = jnp.max(jnp.where(mine_named, table & 3, -1), axis=1)
    named = jnp.where(source == me - 1, 0, jnp.where(source == me + 1, QB - 1, named))
    named = jnp.where(me == 0, 0, jnp.where(me == SEQ - 1, QB - 1, named))
    named = jnp.where(source == me, -1, named)
    by_source = jnp.max(
        jnp.where(source[None, :] == place[:, None], named[None, :], -1), axis=1
    )
    extra_at = jnp.where(me == 0, QB - 1, jnp.where(me == SEQ - 1, 0, -1))
    target = jnp.concatenate([by_source, extra_at[None]]).astype(jnp.int32)

    base = own[:ROWS] + edge_mine + edge_core[0].astype(f32) + edge_across.astype(f32)
    key_grad, value_grad = call(
        sum_kernel,
        [((ROWS, D), bf16), ((ROWS, D), bf16)],
        [target, extra, base, recv],
        12,
        scalars=1,
        scratch=[pltpu.VMEM((ROWS, 2 * D), f32)],
        flops=1 << 20,
        bytes_accessed=4 << 20,
    )

    low = jnp.where(my_x == 0, oq_here, oq_other)
    high = jnp.where(my_x == 0, oq_other, oq_here)

    rows = jax.ShapeDtypeStruct((ROWS, HEADS * D), bf16)
    attended, query_grad = pl.pallas_call(
        put_kernel,
        out_shape=[rows, rows],
        in_specs=[smem, vmem, vmem, anywhere, anywhere],
        out_specs=[anywhere, anywhere],
        input_output_aliases={3: 0, 4: 1},
        scratch_shapes=[pltpu.SemaphoreType.DMA((2, 2))],
        compiler_params=pltpu.CompilerParams(vmem_limit_bytes=8 * MIB),
        cost_estimate=pl.CostEstimate(flops=0, bytes_accessed=1 << 20, transcendentals=0),
    )(info, low, high, attended, query_grad)
    return attended, query_grad, key_grad, value_grad


def solution(mesh):
    rows = P("seq", "head")
    return jax.shard_map(
        local,
        mesh=mesh,
        in_specs=(rows, rows, rows, rows, P("seq", None)),
        out_specs=(rows, rows, rows, rows),
        check_vma=False,
    )
```

```python
import functools
import math

import jax
import jax.numpy as jnp
from jax import lax
from jax.experimental import pallas as pl
from jax.experimental.pallas import tpu as pltpu
from jax.sharding import PartitionSpec as P

D = 128
B = 128
SEQ = 32
ZN = 8
QB = 4
NB = SEQ * QB
HEADS = 8
ROWS = QB * B
PIECE = ROWS + 16
SLOTS = 8
KEYS = SLOTS * B
SCALE = 1.0 / math.sqrt(D)
LOG2E = math.log2(math.e)
FAR = -1e30
MIB = 1 << 20
NT = (((1,), (1,)), ((), ()))
TN = (((0,), (0,)), ((), ()))


def device_of(x, z, c):
    return x * 16 + (z % ZN) * 2 + c


ALL = [(x, z, c) for x in range(2) for z in range(ZN) for c in range(2)]


CORE = [(i, i ^ 1) for i in range(SEQ)]
ACROSS = [(i, i ^ 16) for i in range(SEQ)]
Z_GROUPS = [[device_of(x, z, c) for z in range(ZN)] for x in range(2) for c in range(2)]
ZC_GROUPS = [[device_of(x, z, c) for z in range(ZN) for c in range(2)] for x in range(2)]
EDGE_Z = (0, ZN - 1)
EDGE_ACROSS = [(0, 16), (31, 15)]


def from_edge(step, across):
    return [
        (0, device_of(across, step, 0)),
        (SEQ - 1, device_of(1 - across, ZN - 1 - step, 1)),
    ]


def edge_tree(step):
    pairs = []
    for x in range(2):
        for c, sign in ((0, 1), (1, -1)):
            for r in range(0, ZN, 2 * step):
                ends = [EDGE_Z[c] + sign * r, EDGE_Z[c] + sign * (r + step)]
                pairs.append(tuple(device_of(x, z, c) for z in ends))
    return pairs


def to_edge(step):
    return [
        (device_of(x, EDGE_Z[c] + sign * step, c), device_of(x, EDGE_Z[c], c))
        for x in range(2)
        for c, sign in ((0, 1), (1, -1))
    ]


def reverse(pairs):
    return [(b, a) for a, b in pairs]


def place_of(source, my_x):
    return ((source & 15) << 1) | ((source >> 4) ^ my_x)


def permute(value, pairs):
    return lax.ppermute(value, "seq", pairs)


def dot(a, b, dims=(((1,), (0,)), ((), ()))):
    return lax.dot_general(a, b, dims, preferred_element_type=jnp.float32)


def two_heads(ref_value, first):
    return jnp.concatenate(
        [ref_value[:, first : first + D], ref_value[:, first + D : first + 2 * D]], axis=0
    )


def pack_kernel(ids_ref, k_ref, v_ref, q_ref, g_ref, mine_ref, own_ref, other_ref, sems):
    me = lax.axis_index("seq")
    start = pl.multiple_of((me & 1) * (ROWS - B), B)
    copies = []
    for side, out in enumerate((own_ref, other_ref)):
        first = pl.multiple_of(((me >> 4) ^ side) * (4 * D), D)
        for n, rows in enumerate((q_ref, g_ref)):
            copies.append(
                pltpu.make_async_copy(
                    rows.at[pl.ds(start, B), pl.ds(first, 4 * D)],
                    out.at[:, pl.ds(n * 4 * D, 4 * D)],
                    sems.at[side, n],
                )
            )
    for copy in copies:
        copy.start()
    mine_ref[:ROWS, :D] = k_ref[...]
    mine_ref[:ROWS, D:] = v_ref[...]
    shape = (PIECE - ROWS, 2 * D)
    column = lax.broadcasted_iota(jnp.int32, shape, 1)
    ids = jnp.zeros(shape, jnp.int32)
    for n in range(QB * 3):
        ids = jnp.where(column == n, ids_ref[n // 3, n % 3], ids)
    mine_ref[ROWS:, :] = ids.astype(jnp.float32).astype(jnp.bfloat16)
    for copy in copies:
        copy.wait()


def put_kernel(info, low_ref, high_ref, out_in, dq_in, out_ref, dq_ref, sems):
    me = info[12]
    start = pl.multiple_of((me & 1) * (ROWS - B), B)
    copies = []
    for side, half in enumerate((low_ref, high_ref)):
        for n, rows in enumerate((out_ref, dq_ref)):
            copies.append(
                pltpu.make_async_copy(
                    half.at[:, pl.ds(n * 4 * D, 4 * D)],
                    rows.at[pl.ds(start, B), pl.ds(side * 4 * D, 4 * D)],
                    sems.at[side, n],
                )
            )

    @pl.when(jnp.logical_or(me == 0, me == SEQ - 1))
    def _():
        for copy in copies:
            copy.start()
        for copy in copies:
            copy.wait()


def near_pieces(both_ref, core_ref):
    return [
        (ref[at : at + ROWS, :D], ref[at : at + ROWS, D:])
        for ref in (both_ref, core_ref)
        for at in (0, PIECE)
    ]


def edge_stats_kernel(edge_ref, both_ref, other_ref, stats_ref):
    near = near_pieces(both_ref, other_ref)
    stats_ref[...] = jnp.zeros_like(stats_ref)
    for pair in range(2):
        q2 = two_heads(edge_ref, pair * 2 * D)
        g2 = two_heads(edge_ref, 4 * D + pair * 2 * D)
        scores = [dot(keys, q2, NT) * (SCALE * LOG2E) for keys, _ in near]
        top = scores[0].max(axis=0, keepdims=True)
        for s in scores[1:]:
            top = jnp.maximum(top, s.max(axis=0, keepdims=True))
        total = jnp.zeros_like(top)
        delta = jnp.zeros_like(top)
        for s, (_, values) in zip(scores, near):
            e = jnp.exp2(s - top)
            total = total + e.sum(axis=0, keepdims=True)
            w = dot(values, g2, NT)
            delta = delta + (e * w).sum(axis=0, keepdims=True)
        cols = slice(pair * 2 * D, (pair + 1) * 2 * D)
        stats_ref[0:1, cols] = top
        stats_ref[1:2, cols] = total
        stats_ref[2:3, cols] = delta


def edge_grad_kernel(
    edge_ref, both_ref, other_ref, stats_ref, oq_ref, own_ref, core_ref, across_ref
):
    stats = [stats_ref[n] for n in range(ZN)]
    top = stats[0][0:1]
    for s in stats[1:]:
        top = jnp.maximum(top, s[0:1])
    total = jnp.zeros_like(top)
    delta = jnp.zeros_like(top)
    for s in stats:
        factor = jnp.exp2(s[0:1] - top)
        total = total + s[1:2] * factor
        delta = delta + s[2:3] * factor
    delta = delta / total
    shift = top + jnp.log2(total)
    q_all = jnp.concatenate([two_heads(edge_ref, 0), two_heads(edge_ref, 2 * D)], axis=0)
    g_all = jnp.concatenate([two_heads(edge_ref, 4 * D), two_heads(edge_ref, 6 * D)], axis=0)
    out = None
    for n, (keys, values) in enumerate(near_pieces(both_ref, other_ref)):
        p = jnp.exp2(dot(keys, q_all, NT) * (SCALE * LOG2E) - shift)
        ds = (p * (dot(values, g_all, NT) - delta)).astype(jnp.bfloat16)
        p = p.astype(jnp.bfloat16)
        o = dot(values, p, TN)
        dq = dot(keys, ds, TN)
        out = (o, dq) if out is None else (out[0] + o, out[1] + dq)
        dk = dot(ds, q_all) * SCALE
        dv = dot(p, g_all)
        if n == 0:
            own_ref[:, :D] = dk
            own_ref[:, D:] = dv
        elif n == 1:
            across_ref[:, :D] = dk
            across_ref[:, D:] = dv
        else:
            core_ref[n - 2, :, :D] = dk.astype(jnp.bfloat16)
            core_ref[n - 2, :, D:] = dv.astype(jnp.bfloat16)
    for h in range(4):
        cols = slice(h * D, (h + 1) * D)
        oq_ref[:, cols] = out[0][:, cols].T.astype(jnp.bfloat16)
        oq_ref[:, 4 * D + h * D : 4 * D + (h + 1) * D] = (out[1][:, cols].T * SCALE).astype(
            jnp.bfloat16
        )


def middle_kernel(info, q_ref, g_ref, all_ref, _, *refs):
    out_ref, dq_ref, send_ref, state_ref, side_ref = refs[:5]
    kv, s_ref, e_all, ds_all, slots, sems, slot_sems = refs[5:]
    me = info[12]
    step = pl.program_id(0)
    last_step = step == QB // 2 - 1
    buffer = step & 1

    def fetch(block, at, half, slot):
        block = jnp.clip(block, 0, NB - 1)
        place = place_of(block >> 2, me >> 4)
        row = pl.multiple_of(place * PIECE + (block & 3) * B, 16)
        return pltpu.make_async_copy(
            all_ref.at[pl.ds(row, B), :],
            kv.at[at, half, pl.ds(slot * B, B), :],
            sems.at[at, half, slot],
        )

    def slot_copy(at, which, destination):
        return pltpu.make_async_copy(
            slots.at[at, which], send_ref.at[destination], slot_sems.at[at, which]
        )

    def fetch_all(first, at):
        for half in range(2):
            block = me * QB + first + half
            for slot, name in enumerate((block - 1, block, block + 1, 0, NB - 1)):
                fetch(jnp.int32(name), at, half, slot).start()
            for r in range(3):
                fetch(info[(first + half) * 3 + r], at, half, 5 + r).start()

    @pl.when(step == 0)
    def _():
        fetch_all(0, 0)
        state_ref[...] = jnp.zeros_like(state_ref)
        side_ref[...] = jnp.zeros_like(side_ref)

    @pl.when(jnp.logical_not(last_step))
    def _():
        fetch_all(2, 1)

    for half in range(2):
        for slot in range(SLOTS):
            fetch(jnp.int32(0), buffer, half, slot).wait()

    pairs = range(HEADS // 2)
    heads = [[slice((2 * p + h) * D, (2 * p + h + 1) * D) for h in range(2)] for p in pairs]
    chunks = [slice(n * B, (n + 1) * B) for n in range(KEYS // B)]

    def work(half):
        block = me * QB + 2 * step + half
        low_bias = jnp.where(block == 1, FAR, 0.0).astype(jnp.float32)
        high_bias = jnp.where(block == NB - 2, FAR, 0.0).astype(jnp.float32)
        rows = slice(half * B, (half + 1) * B)
        scaled_q, scaled_g = [], []

        def scores(pair):
            q_t = jnp.concatenate([q_ref[rows, h].T for h in heads[pair]], axis=1)
            top = None
            for n, c in enumerate(chunks):
                s = dot(kv[buffer, half, c, :D], q_t)
                if n == 0:
                    s = s + low_bias
                if n == 2:
                    s = s + high_bias
                s_ref[pair % 2, c, :] = s
                m = s.max(axis=0, keepdims=True)
                top = m if top is None else jnp.maximum(top, m)
            return top * (SCALE * LOG2E)

        def weights(pair, top):
            cols = slice(pair * 2 * D, (pair + 1) * 2 * D)
            total = None
            for c in chunks:
                e = jnp.exp2(s_ref[pair % 2, c, :] * (SCALE * LOG2E) - top)
                e_all[half, c, cols] = e.astype(jnp.bfloat16)
                t = e.sum(axis=0, keepdims=True)
                total = t if total is None else total + t
            return 1.0 / total

        def gradients(pair, part):
            cols = slice(pair * 2 * D, (pair + 1) * 2 * D)
            g_t = jnp.concatenate([g_ref[rows, h].T for h in heads[pair]], axis=1)
            o = dot(values_t, e_all[half, :, cols]) * part
            delta = (g_t.astype(jnp.float32) * o).sum(axis=0, keepdims=True)
            for c in chunks:
                e = e_all[half, c, cols].astype(jnp.float32)
                ds = e * (dot(kv[buffer, half, c, D:], g_t) - delta)
                ds_all[half, c, cols] = ds.astype(jnp.bfloat16)
            dq = dot(keys_t, ds_all[half, :, cols]) * (part * SCALE)
            for n, h in enumerate(heads[pair]):
                one = slice(n * B, (n + 1) * B)
                out_ref[rows, h] = o[:, one].T.astype(jnp.bfloat16)
                dq_ref[rows, h] = dq[:, one].T.astype(jnp.bfloat16)
                column = part[:, one].T
                scaled_q.append((q_ref[rows, h] * (column * SCALE)).astype(jnp.bfloat16))
                scaled_g.append((g_ref[rows, h] * column).astype(jnp.bfloat16))

        top = scores(0)
        yield None
        values_t = kv[buffer, half, :, D:].T
        keys_t = kv[buffer, half, :, :D].T
        for pair in pairs:
            part = weights(pair, top)
            if pair + 1 < HEADS // 2:
                top = scores(pair + 1)
            gradients(pair, part)
        yield None
        dk = dot(ds_all[half], jnp.concatenate(scaled_q, axis=0))
        dv = dot(e_all[half], jnp.concatenate(scaled_g, axis=0))
        yield dk, dv

    first, second = work(0), work(1)
    next(first)
    next(first)
    next(second)
    results = [next(first)]
    next(second)
    results.append(next(second))

    def add(half):
        j = 2 * step + half
        block = me * QB + j
        middle = jnp.logical_and(block > 0, block < NB - 1)
        to_low = jnp.logical_and(jnp.logical_and(middle, j == 0), me != 1)
        to_high = jnp.logical_and(jnp.logical_and(middle, j == QB - 1), me != SEQ - 2)
        dk, dv = results[half]

        def contribution(slot):
            rows = slice(slot * B, (slot + 1) * B)
            return jnp.concatenate([dk[rows], dv[rows]], axis=1)

        def low(slot):
            return contribution(slot).astype(jnp.bfloat16)

        @pl.when(middle)
        def _():
            state_ref[pl.ds(pl.multiple_of(j * B, B), B), :] += contribution(1)
            state_ref[ROWS : ROWS + B, :] += contribution(3)
            state_ref[ROWS + B :, :] += contribution(4)

            @pl.when(j > 0)
            def _():
                state_ref[pl.ds(pl.multiple_of((j - 1) * B, B), B), :] += contribution(0)

            @pl.when(j < QB - 1)
            def _():
                state_ref[pl.ds(pl.multiple_of((j + 1) * B, B), B), :] += contribution(2)

            for r in range(3):
                slots[j, r] = low(5 + r)
                slot_copy(j, r, info[j * 3 + r] >> 2).start()

            @pl.when(j == 0)
            def _():
                slots[j, 3] = low(0)

            @pl.when(j == QB - 1)
            def _():
                slots[j, 3] = low(2)

            @pl.when(to_low)
            def _():
                slot_copy(j, 3, me - 1).start()

            @pl.when(to_high)
            def _():
                slot_copy(j, 3, me + 1).start()

            @pl.when(jnp.logical_and(j == 0, me == 1))
            def _():
                side_ref[...] = low(0)

            @pl.when(jnp.logical_and(j == QB - 1, me == SEQ - 2))
            def _():
                side_ref[...] = low(2)

        def finish():
            @pl.when(middle)
            def _():
                for r in range(3):
                    slot_copy(j, r, 0).wait()

            @pl.when(jnp.logical_or(to_low, to_high))
            def _():
                slot_copy(j, 3, 0).wait()

        return finish

    finishes = [add(0), add(1)]

    @pl.when(last_step)
    def _():
        slots[QB, 0] = state_ref[ROWS : ROWS + B, :].astype(jnp.bfloat16)
        slots[QB, 1] = state_ref[ROWS + B :, :].astype(jnp.bfloat16)

        @pl.when(me == 0)
        def _():
            state_ref[:B, :] += state_ref[ROWS : ROWS + B, :]

        @pl.when(me != 0)
        def _():
            slot_copy(QB, 0, 0).start()
            slot_copy(QB, 0, 0).wait()

        @pl.when(me == SEQ - 1)
        def _():
            state_ref[ROWS - B : ROWS, :] += state_ref[ROWS + B :, :]

        @pl.when(me != SEQ - 1)
        def _():
            slot_copy(QB, 1, SEQ - 1).start()
            slot_copy(QB, 1, SEQ - 1).wait()

    for finish in finishes:
        finish()


def middle_call(info, query_rows, out_grad, gathered, later):
    bf16, f32 = jnp.bfloat16, jnp.float32
    anywhere = pl.BlockSpec(memory_space=pl.ANY)
    whole = pl.BlockSpec(memory_space=pltpu.VMEM)
    rows = pl.BlockSpec((2 * B, HEADS * D), lambda step: (step, 0))
    return pl.pallas_call(
        middle_kernel,
        grid=(QB // 2,),
        out_shape=[
            jax.ShapeDtypeStruct((ROWS, HEADS * D), bf16),
            jax.ShapeDtypeStruct((ROWS, HEADS * D), bf16),
            jax.ShapeDtypeStruct((SEQ, B, 2 * D), bf16),
            jax.ShapeDtypeStruct((ROWS + 2 * B, 2 * D), f32),
            jax.ShapeDtypeStruct((B, 2 * D), bf16),
        ],
        in_specs=[pl.BlockSpec(memory_space=pltpu.SMEM), rows, rows, anywhere, anywhere],
        out_specs=[rows, rows, anywhere, whole, whole],
        scratch_shapes=[
            pltpu.VMEM((2, 2, KEYS, 2 * D), bf16),
            pltpu.VMEM((2, KEYS, 2 * D), f32),
            pltpu.VMEM((2, KEYS, HEADS * B), bf16),
            pltpu.VMEM((2, KEYS, HEADS * B), bf16),
            pltpu.VMEM((QB + 1, 4, B, 2 * D), bf16),
            pltpu.SemaphoreType.DMA((2, 2, SLOTS)),
            pltpu.SemaphoreType.DMA((QB + 1, 4)),
        ],
        compiler_params=pltpu.CompilerParams(vmem_limit_bytes=56 * MIB),
        cost_estimate=pl.CostEstimate(
            flops=QB * 6 * 2 * KEYS * HEADS * B * D,
            bytes_accessed=QB * (4 << 20),
            transcendentals=QB * KEYS * HEADS * B,
        ),
    )(info, query_rows, out_grad, gathered, later)


def sum_kernel(target, extra_ref, base_ref, recv_ref, dk_ref, dv_ref, acc):
    acc[...] = base_ref[...]
    t = target[SEQ]

    @pl.when(t >= 0)
    def _():
        rows = pl.ds(pl.multiple_of(t * B, B), B)
        acc[rows, :] += extra_ref[...].astype(jnp.float32)

    def add(s, carry):
        t = target[s]

        @pl.when(t >= 0)
        def _():
            rows = pl.ds(pl.multiple_of(t * B, B), B)
            acc[rows, :] += recv_ref[s].astype(jnp.float32)

        return carry

    lax.fori_loop(0, SEQ, add, 0)
    dk_ref[...] = acc[:, :D].astype(jnp.bfloat16)
    dv_ref[...] = acc[:, D:].astype(jnp.bfloat16)


def call(
    kernel, outs, args, vmem_mib, scalars=0, later=0, scratch=(), flops=0, bytes_accessed=0, exps=0
):
    vmem = pl.BlockSpec(memory_space=pltpu.VMEM)
    smem = pl.BlockSpec(memory_space=pltpu.SMEM)
    return pl.pallas_call(
        kernel,
        out_shape=[jax.ShapeDtypeStruct(shape, dtype) for shape, dtype in outs],
        in_specs=[smem] * scalars
        + [vmem] * (len(args) - scalars - later)
        + [pl.BlockSpec(memory_space=pl.ANY)] * later,
        out_specs=[vmem] * len(outs),
        scratch_shapes=list(scratch),
        compiler_params=pltpu.CompilerParams(vmem_limit_bytes=vmem_mib * MIB),
        cost_estimate=pl.CostEstimate(
            flops=flops, bytes_accessed=bytes_accessed, transcendentals=exps
        ),
    )(*args)


def hold(*values):
    return lax.optimization_barrier(values)


def local(query_rows, key_rows, value_rows, out_grad, random_blocks):
    bf16, f32 = jnp.bfloat16, jnp.float32
    me = lax.axis_index("seq").astype(jnp.int32)
    my_x, my_z, my_c = me >> 4, (me >> 1) & 7, me & 1
    ids = random_blocks.reshape(QB * 3).astype(jnp.int32)

    is_root = jnp.logical_or(me == 0, me == SEQ - 1)
    info = jnp.concatenate([ids, me[None], jnp.zeros((3,), jnp.int32)])
    smem = pl.BlockSpec(memory_space=pltpu.SMEM)
    vmem = pl.BlockSpec(memory_space=pltpu.VMEM)
    anywhere = pl.BlockSpec(memory_space=pl.ANY)
    mine, edge_own, edge_other = pl.pallas_call(
        pack_kernel,
        out_shape=[
            jax.ShapeDtypeStruct((PIECE, 2 * D), bf16),
            jax.ShapeDtypeStruct((B, 8 * D), bf16),
            jax.ShapeDtypeStruct((B, 8 * D), bf16),
        ],
        in_specs=[smem, vmem, vmem, anywhere, anywhere],
        out_specs=[vmem, vmem, vmem],
        scratch_shapes=[pltpu.SemaphoreType.DMA((2, 2))],
        compiler_params=pltpu.CompilerParams(vmem_limit_bytes=56 * MIB),
        cost_estimate=pl.CostEstimate(flops=0, bytes_accessed=2 << 20, transcendentals=0),
    )(random_blocks, key_rows, value_rows, query_rows, out_grad)
    partner = permute(mine, ACROSS)

    edge = jnp.where(is_root, edge_own, jnp.zeros_like(edge_own))
    edge = edge + permute(edge_other, from_edge(0, 1))
    edge = edge + permute(edge_own, from_edge(4, 0))
    edge = edge + permute(edge_other, from_edge(4, 1))
    both, edge = hold(jnp.concatenate([mine, partner], axis=0), edge)
    gathered = lax.all_gather(both, "seq", axis_index_groups=ZC_GROUPS, tiled=True)
    near = [both, permute(both, CORE)]
    for step in (2, 1):
        edge = edge + permute(edge, edge_tree(step))

    edge_flops = 2 * 4 * ROWS * ROWS * D
    (stats,) = call(
        edge_stats_kernel,
        [((8, 4 * D), f32)],
        [edge] + near,
        24,
        flops=2 * edge_flops,
        bytes_accessed=2 << 20,
        exps=4 * ROWS * ROWS,
    )
    all_stats = lax.all_to_all(
        jnp.broadcast_to(stats, (ZN, *stats.shape)), "seq", 0, 0, axis_index_groups=Z_GROUPS
    )
    edge_oq, edge_mine, edge_core, edge_across = call(
        edge_grad_kernel,
        [
            ((B, 8 * D), bf16),
            ((ROWS, 2 * D), f32),
            ((2, ROWS, 2 * D), bf16),
            ((ROWS, 2 * D), f32),
        ],
        [edge] + near + [all_stats],
        24,
        flops=6 * edge_flops,
        bytes_accessed=4 << 20,
        exps=4 * ROWS * ROWS,
    )
    edge_core = permute(edge_core, CORE)
    oq_sum = edge_oq.astype(f32)
    oq_sum = oq_sum + permute(edge_oq, reverse(edge_tree(1))).astype(f32)
    oq_low = oq_sum.astype(bf16)
    oq_far = [permute(oq_low, to_edge(step)) for step in (4, 6, 2)]
    edge_across = permute((edge_across + edge_core[1].astype(f32)).astype(bf16), ACROSS)

    attended, query_grad, send, own, extra = middle_call(
        info, query_rows, out_grad, gathered, oq_low
    )

    *oq_far, edge_across, send = hold(*oq_far, edge_across, send)
    for part in oq_far:
        oq_sum = oq_sum + part.astype(f32)
    oq_here = oq_sum.astype(bf16)
    oq_other = permute(oq_here, reverse(EDGE_ACROSS))
    extra = permute(extra, [(1, 0), (SEQ - 2, SEQ - 1)])
    recv = lax.all_to_all(send, "seq", 0, 0)

    table = gathered.reshape(SEQ, PIECE, 2 * D)[:, ROWS, : QB * 3].astype(jnp.int32)
    place = jnp.arange(SEQ, dtype=jnp.int32)
    source = (place >> 1) | (((place & 1) ^ my_x) << 4)
    row = source[:, None] * QB + jnp.arange(QB * 3, dtype=jnp.int32)[None, :] // 3
    read = jnp.logical_and(row > 0, row < NB - 1)
    mine_named = jnp.logical_and((table >> 2) == me, read)
    named = jnp.max(jnp.where(mine_named, table & 3, -1), axis=1)
    named = jnp.where(source == me - 1, 0, jnp.where(source == me + 1, QB - 1, named))
    named = jnp.where(me == 0, 0, jnp.where(me == SEQ - 1, QB - 1, named))
    named = jnp.where(source == me, -1, named)
    by_source = jnp.max(
        jnp.where(source[None, :] == place[:, None], named[None, :], -1), axis=1
    )
    extra_at = jnp.where(me == 0, QB - 1, jnp.where(me == SEQ - 1, 0, -1))
    target = jnp.concatenate([by_source, extra_at[None]]).astype(jnp.int32)

    base = own[:ROWS] + edge_mine + edge_core[0].astype(f32) + edge_across.astype(f32)
    key_grad, value_grad = call(
        sum_kernel,
        [((ROWS, D), bf16), ((ROWS, D), bf16)],
        [target, extra, base, recv],
        12,
        scalars=1,
        scratch=[pltpu.VMEM((ROWS, 2 * D), f32)],
        flops=1 << 20,
        bytes_accessed=4 << 20,
    )

    low = jnp.where(my_x == 0, oq_here, oq_other)
    high = jnp.where(my_x == 0, oq_other, oq_here)

    rows = jax.ShapeDtypeStruct((ROWS, HEADS * D), bf16)
    attended, query_grad = pl.pallas_call(
        put_kernel,
        out_shape=[rows, rows],
        in_specs=[smem, vmem, vmem, anywhere, anywhere],
        out_specs=[anywhere, anywhere],
        input_output_aliases={3: 0, 4: 1},
        scratch_shapes=[pltpu.SemaphoreType.DMA((2, 2))],
        compiler_params=pltpu.CompilerParams(vmem_limit_bytes=8 * MIB),
        cost_estimate=pl.CostEstimate(flops=0, bytes_accessed=1 << 20, transcendentals=0),
    )(info, low, high, attended, query_grad)
    return attended, query_grad, key_grad, value_grad


def solution(mesh):
    rows = P("seq", "head")
    return jax.shard_map(
        local,
        mesh=mesh,
        in_specs=(rows, rows, rows, rows, P("seq", None)),
        out_specs=(rows, rows, rows, rows),
        check_vma=False,
    )
```
